256 devices in a mesh: replica: 4 (over z_hi), fsdp: 64 (over z_lo, y, x, core).
Axes of the slice: x: 4, y: 4, z: 8 (z_hi: 4, z_lo: 2; z = z_hi * 2 + z_lo), core: 2. Of those that a mesh axis runs over, the one named last changes fastest.
Arguments:
- hidden: bfloat16 [4, 24576, 8192], P('replica', 'fsdp'), may hold values from -6 to 6
- master: float32 [4, 8192, 512], P('replica', 'fsdp'), may hold values from -0.0625 to 0.0625
- moment_first: float32 [4, 8192, 512], P('replica', 'fsdp'), may hold values from -4 to 4
- moment_second: float32 [4, 8192, 512], P('replica', 'fsdp'), may hold values from 0.05 to 2
- key_grad: bfloat16 [4, 24576, 512], P('replica', 'fsdp'), may hold values from -0.09375 to 0.09375
- frag_global: float32 [2, 8388608], P(None, 'fsdp'), may hold values from -6 to 6
- frag_local: float32 [4, 2, 8388608], P('replica', None, 'fsdp'), may hold values from -6 to 6
- frag_moment: float32 [2, 8388608], P(None, 'fsdp'), may hold values from -6 to 6
- frag_index: int32 [1], replicated, may hold values from 0 to 1
Outputs:
- new_master: float32 [4, 8192, 512], P('replica', 'fsdp')
- new_first: float32 [4, 8192, 512], P('replica', 'fsdp')
- new_second: float32 [4, 8192, 512], P('replica', 'fsdp')
- outer_global: float32 [8388608], P('fsdp')
- outer_moment: float32 [8388608], P('fsdp')
- mixed_local: float32 [4, 8388608], P('replica', 'fsdp')
The draws below stay inside these ranges and needn't reach their ends.
All inputs are finite; a program needn't handle non-finite values.
Results may differ from the reference program's by a relative error of at most 0.0011.
Values may be sent and summed in bfloat16 or wider, within the bound.
A program may use at most 128 MiB of HBM per device.

```python
import math
import jax
import jax.numpy as jnp
from jax import lax

D = 8192
HEAD = 128
KV = 512
TOK_DEV = 384
TOKENS = 24576
FRAGS = 2
FRAG = 8388608
REPLICAS = 4
N_FSDP = 64


def block_scale(key, dims, cuts, low, high):
    def one(dim, blocks):
        steps = jax.random.uniform(jax.random.fold_in(jax.random.fold_in(key, 6), dim), (blocks,), jnp.float32, low / len(cuts), high / len(cuts))
        return jnp.repeat(jnp.exp(steps), dims[dim] // blocks).reshape((-1,) + (1,) * (len(dims) - dim - 1))

    factor_of = one(*cuts[0])
    for cut in cuts[1:]:
        factor_of = factor_of * one(*cut)
    return factor_of


def noise(key, dims, width, most, split=(), held_as=jnp.bfloat16):
    array = jax.random.normal(key, dims, jnp.float32) * width
    if len(split) > 0:
        array = block_scale(key, dims, split, -0.22, 0.18) * array
    return jnp.clip(array, min=-most, max=most).astype(held_as)


def setup_inputs(seed: int = 0) -> dict:
    key_of = jax.random.split(jax.random.key(seed), 10)
    hidden = noise(key_of[0], (REPLICAS, TOKENS, D), 1.0, 6.0, ((0, 4), (1, 64)))
    master = noise(key_of[1], (REPLICAS, D, KV), D ** -0.5, 0.0625, ((0, 4), (1, 64)), jnp.float32)
    moment_first = noise(key_of[2], (REPLICAS, D, KV), 0.3, 4.0, ((0, 4), (1, 64)), jnp.float32)
    moment_second = jnp.clip(jnp.exp(math.log(2.0) - 3.6888794 * jax.random.uniform(key_of[3], (REPLICAS, D, KV), jnp.float32) ** block_scale(key_of[3], (REPLICAS, D, KV), ((0, 4), (1, 64)), -0.2, 0.2)), 0.05, 2.0)
    key_grad = noise(key_of[4], (REPLICAS, TOKENS, KV), ((TOK_DEV * N_FSDP) ** -0.5), 0.09375, ((0, 4), (1, 64)))
    frag_global = noise(key_of[5], (FRAGS, FRAG), 1.0, 6.0, ((1, 64),), jnp.float32)
    frag_local = noise(key_of[6], (REPLICAS, FRAGS, FRAG), 1.0, 6.0, ((0, 4), (2, 64)), jnp.float32)
    frag_moment = noise(key_of[7], (FRAGS, FRAG), 0.5, 6.0, ((1, 64),), jnp.float32)
    frag_index = jax.random.randint(key_of[8], (1,), 0, FRAGS).astype(jnp.int32)
    return {"hidden": hidden, "master": master, "moment_first": moment_first, "moment_second": moment_second, "key_grad": key_grad, "frag_global": frag_global, "frag_local": frag_local, "frag_moment": frag_moment, "frag_index": frag_index}


def norm_backward(keys, grads):
    count = keys.shape[0]
    shaped = keys.reshape(count, -1, HEAD)
    inverse = lax.rsqrt(lax.optimization_barrier(jnp.mean(shaped * shaped, axis=-1, keepdims=True)) + 1e-06)
    normed = shaped * inverse
    upstream = grads.astype(jnp.float32).reshape(count, -1, HEAD)
    result = inverse * (upstream - normed * lax.optimization_barrier(jnp.mean(upstream * normed, axis=-1, keepdims=True)))
    return result.reshape(count, -1).astype(jnp.bfloat16)

def adamw(weights, first, second, grad):
    first_new = 0.9 * first + 0.1 * grad
    second_new = 0.95 * second + 0.05 * grad * grad
    first_hat = first_new / (1.0 - 0.9 ** 10)
    second_hat = second_new / (1.0 - 0.95 ** 10)
    weights_new = weights - 0.01 * (first_hat / (jnp.sqrt(second_hat) + 1e-08) + 0.1 * weights)
    return (weights_new, first_new, second_new)

def reference(hidden, master, moment_first, moment_second, key_grad, frag_global, frag_local, frag_moment, frag_index):
    masters, firsts, seconds = ([], [], [])
    for replica in range(REPLICAS):
        weight_bf = master[replica].astype(jnp.bfloat16)
        keys = jnp.dot(hidden[replica], weight_bf, preferred_element_type=jnp.float32)
        key_delta = norm_backward(keys, key_grad[replica])
        grad = jnp.dot(hidden[replica].T, key_delta, preferred_element_type=jnp.float32)
        weights_new, first_new, second_new = adamw(master[replica], moment_first[replica], moment_second[replica], grad)
        masters.append(weights_new)
        firsts.append(first_new)
        seconds.append(second_new)
    chosen = frag_index[0].astype(jnp.int32)
    glob = lax.dynamic_index_in_dim(frag_global, chosen, 0, keepdims=False)
    moment = lax.dynamic_index_in_dim(frag_moment, chosen, 0, keepdims=False)
    local = lax.dynamic_index_in_dim(frag_local, chosen, 1, keepdims=False)
    delta = lax.optimization_barrier(jnp.sum(glob[None, :] - local, axis=0)) / REPLICAS
    outer_moment = 0.9 * moment + delta
    outer_global = glob - 0.7 * (0.9 * outer_moment + delta)
    mixed_local = 0.5 * local + 0.5 * outer_global[None, :]
    return (jnp.stack(masters), jnp.stack(firsts), jnp.stack(seconds), outer_global, outer_moment, mixed_local)
```

```python
import functools

import jax
import jax.numpy as jnp
from jax import lax
from jax.experimental import pallas as pl
from jax.experimental.pallas import tpu as pltpu
from jax.sharding import PartitionSpec as P

MESH = pl.DeviceIdType.MESH
HEAD = 128
PARTS = 2
WIDE = 256
TOK = 384
ROWS = 128
MESSAGES = 256


def adamw(weights, first, second, grad):
    first_new = 0.9 * first + 0.1 * grad
    second_new = 0.95 * second + 0.05 * grad * grad
    first_hat = first_new / (1.0 - 0.9**10)
    second_hat = second_new / (1.0 - 0.95**10)
    weights_new = weights - 0.01 * (first_hat / (jnp.sqrt(second_hat) + 1e-08) + 0.1 * weights)
    return (weights_new, first_new, second_new)


def norm_backward(keys, upstream):
    inverse = lax.rsqrt(jnp.mean(keys * keys, axis=-1, keepdims=True) + 1e-06)
    normed = keys * inverse
    return inverse * (upstream - normed * jnp.mean(upstream * normed, axis=-1, keepdims=True))


def kernel(
    hidden,
    master,
    key_grad,
    diff,
    grad_out,
    delta_out,
    hid,
    wts,
    acc,
    acc_in,
    dlt,
    stage,
    stage_in,
    row,
    final,
    z_stage,
    z_in,
    rep_in,
    send_sem,
    recv_sem,
    hid_sem,
):
    r = lax.axis_index("replica")
    f = lax.axis_index("fsdp")
    z, y, x, c = f // 32, (f // 8) % 4, (f // 2) % 4, f % 2

    def at(zz, yy, xx, cc):
        return (r, zz * 32 + (yy % 4) * 8 + (xx % 4) * 2 + cc)

    a_up, a_down = at(z, y + z, x + 1 - z, c), at(z, y + 4 - z, x + 3 + z, c)
    b_up, b_down = at(z, y + 1 - z, x + z, c), at(z, y + 3 + z, x + 4 - z, c)
    over_z, sibling = at(1 - z, y, x, c), at(z, y, x, 1 - c)
    reps = [((r + k) % 4, f) for k in (1, 2, 3)]
    ways = (((a_up, a_down), (b_up, b_down)), ((b_up, b_down), (a_up, a_down)))

    barrier = pltpu.get_barrier_semaphore()
    peers = [a_up, a_down, b_up, b_down, over_z, sibling, *reps]
    for peer in peers:
        pl.semaphore_signal(barrier, inc=1, device_id=peer, device_id_type=MESH)

    wts[0, 0] = master[:, :WIDE].astype(jnp.bfloat16)
    wts[1, 0] = master[:, WIDE:].astype(jnp.bfloat16)
    pl.semaphore_wait(barrier, len(peers))

    sent = {}

    def send(name, src, dst, to):
        n = len(sent)
        copy = pltpu.make_async_remote_copy(
            src_ref=src,
            dst_ref=dst,
            send_sem=send_sem.at[n],
            recv_sem=recv_sem.at[n],
            device_id=to,
            device_id_type=MESH,
        )
        copy.start()
        sent[name] = copy

    def arrived(*name):
        sent[name].wait_recv()

    def slot(h, t, s, q):
        return wts.at[h, 16 * t + 4 * s + q]

    lower, upper = pl.ds(0, ROWS // 2), pl.ds(ROWS // 2, ROWS // 2)

    def over_second(h, t, q):
        (_, _), (up, down) = ways[t]
        src = slot(h, t, 0, q)
        send(("s+", h, t, q), src, slot(h, t, 3, q), up)
        send(("s-", h, t, q), src, slot(h, t, 1, q), down)

    def gather_own(h, t):
        (up, down), _ = ways[t]
        if t == 1:
            arrived("z", h)
        src = slot(h, t, 0, 0)
        send(("f+", h, t), src, slot(h, t, 0, 3), up)
        send(("f-", h, t), src, slot(h, t, 0, 1), down)
        over_second(h, t, 0)

    def gather_next(h, t):
        (up, down), _ = ways[t]
        arrived("f+", h, t)
        send(("ff+", h, t), slot(h, t, 0, 3).at[lower], slot(h, t, 0, 2).at[lower], up)
        arrived("f-", h, t)
        send(("ff-", h, t), slot(h, t, 0, 1).at[upper], slot(h, t, 0, 2).at[upper], down)
        over_second(h, t, 3)
        over_second(h, t, 1)

    def gather_far(h, t):
        arrived("ff+", h, t)
        arrived("ff-", h, t)
        over_second(h, t, 2)

    def gather_pass(h, t, q):
        _, (up, down) = ways[t]
        arrived("s+", h, t, q)
        send(("ss+", h, t, q), slot(h, t, 3, q).at[lower], slot(h, t, 2, q).at[lower], up)
        arrived("s-", h, t, q)
        send(("ss-", h, t, q), slot(h, t, 1, q).at[upper], slot(h, t, 2, q).at[upper], down)

    def keys_add(h, t, s):
        if s == 2:
            for q in range(4):
                arrived("ss+", h, t, q)
                arrived("ss-", h, t, q)
        first = 16 * t + 4 * s
        part = jnp.dot(
            hid[:, first * ROWS : (first + 4) * ROWS],
            wts[h, first : first + 4].reshape(4 * ROWS, WIDE),
            preferred_element_type=jnp.float32,
        )
        if (t, s) == (0, 0):
            acc[h] = part
        else:
            acc[h] += part

    def keys_swap(h):
        send(("keys", h), acc.at[h, pl.ds(TOK, TOK)], acc_in.at[h], sibling)

    def deltas(h):
        arrived("keys", h)
        for n in range(WIDE // HEAD):
            cols = slice(n * HEAD, (n + 1) * HEAD)
            keys = acc[h, :TOK, cols] + acc_in[h, :, cols]
            at_col = h * WIDE + n * HEAD
            up = key_grad[:, at_col : at_col + HEAD].astype(jnp.float32)
            dlt[h, n * HEAD : (n + 1) * HEAD, :TOK] = norm_backward(keys, up).T.astype(jnp.bfloat16)
        send(("delta", h), dlt.at[h, :, pl.ds(0, TOK)], dlt.at[h, :, pl.ds(TOK, TOK)], sibling)

    low, high = slice(0, WIDE // 2), slice(WIDE // 2, WIDE)

    def grad_row(h, t, s):
        first = 16 * t + 4 * s
        return jnp.dot(
            dlt[h], hid[:, first * ROWS : (first + 4) * ROWS], preferred_element_type=jnp.float32
        )

    def row_send(name, h, t, s, half, to):
        n = 0 if half is low else WIDE // 2
        send(
            (name, h, t),
            stage.at[h, t, s, pl.ds(n, WIDE // 2), :],
            stage_in.at[h, t, s, pl.ds(n, WIDE // 2), :],
            to,
        )

    def scatter_far(h, t):
        _, (up, down) = ways[t]
        stage[h, t, 2] = grad_row(h, t, 2).astype(jnp.bfloat16)
        row_send("rf+", h, t, 2, low, up)
        row_send("rf-", h, t, 2, high, down)

    def scatter_near(h, t):
        _, (up, down) = ways[t]
        g1 = grad_row(h, t, 1)
        stage[h, t, 1, high, :] = g1[high].astype(jnp.bfloat16)
        row_send("r+h", h, t, 1, high, up)
        g3 = grad_row(h, t, 3)
        stage[h, t, 3, low, :] = g3[low].astype(jnp.bfloat16)
        row_send("r-l", h, t, 3, low, down)
        arrived("rf+", h, t)
        stage[h, t, 1, low, :] = (g1[low] + stage_in[h, t, 2, low, :].astype(jnp.float32)).astype(jnp.bfloat16)
        row_send("r+l", h, t, 1, low, up)
        arrived("rf-", h, t)
        stage[h, t, 3, high, :] = (g3[high] + stage_in[h, t, 2, high, :].astype(jnp.float32)).astype(jnp.bfloat16)
        row_send("r-h", h, t, 3, high, down)

    def scatter_own(h, t):
        g0 = grad_row(h, t, 0)
        for name in ("r+h", "r-l", "r+l", "r-h"):
            arrived(name, h, t)
        row[h, t] = g0 + stage_in[h, t, 1].astype(jnp.float32) + stage_in[h, t, 3].astype(jnp.float32)

    def one_send(name, h, t, q, half, to):
        n = 0 if half is low else WIDE // 2
        cols = pl.ds(q * ROWS, ROWS)
        send(
            (name, h, t),
            stage.at[h, t, 0, pl.ds(n, WIDE // 2), cols],
            stage_in.at[h, t, 0, pl.ds(n, WIDE // 2), cols],
            to,
        )

    def cols_of(q):
        return slice(q * ROWS, (q + 1) * ROWS)

    def first_far(h, t):
        (up, down), _ = ways[t]
        stage[h, t, 0, :, cols_of(2)] = row[h, t, :, cols_of(2)].astype(jnp.bfloat16)
        one_send("cf+", h, t, 2, low, up)
        one_send("cf-", h, t, 2, high, down)
        stage[h, t, 0, high, cols_of(1)] = row[h, t, high, cols_of(1)].astype(jnp.bfloat16)
        one_send("c+h", h, t, 1, high, up)
        stage[h, t, 0, low, cols_of(3)] = row[h, t, low, cols_of(3)].astype(jnp.bfloat16)
        one_send("c-l", h, t, 3, low, down)

    def first_near(h, t):
        (up, down), _ = ways[t]
        arrived("cf+", h, t)
        got = stage_in[h, t, 0, low, cols_of(2)].astype(jnp.float32)
        stage[h, t, 0, low, cols_of(1)] = (row[h, t, low, cols_of(1)] + got).astype(jnp.bfloat16)
        one_send("c+l", h, t, 1, low, up)
        arrived("cf-", h, t)
        got = stage_in[h, t, 0, high, cols_of(2)].astype(jnp.float32)
        stage[h, t, 0, high, cols_of(3)] = (row[h, t, high, cols_of(3)] + got).astype(jnp.bfloat16)
        one_send("c-h", h, t, 3, high, down)

    def first_own(h, t):
        for name in ("c+h", "c-l", "c+l", "c-h"):
            arrived(name, h, t)
        got = stage_in[h, t, 0, :, cols_of(1)].astype(jnp.float32) + stage_in[h, t, 0, :, cols_of(3)].astype(jnp.float32)
        total = row[h, t, :, cols_of(0)] + got
        if t == 1:
            z_stage[h] = total
            send(("gz", h), z_stage.at[h], z_in.at[h], over_z)
        else:
            final[h] = total

    def finish(h):
        arrived("gz", h)
        grad_out[h * WIDE : (h + 1) * WIDE, :] = final[h] + z_in[h]

    def replicas_start():
        for k, to in zip((1, 2, 3), reps):
            quarter = pl.ds(((r + k) % 4) * 256, 256)
            send(("rep", k), diff.at[quarter], rep_in.at[k - 1], to)

    def replicas_sum():
        for k in (1, 2, 3):
            arrived("rep", k)
        mine = pl.ds(r * 256, 256)
        delta_out[mine, :] = (diff[mine, :] + rep_in[0] + rep_in[1] + rep_in[2]) * 0.25
        for k, to in zip((1, 2, 3), reps):
            send(("rep out", k), delta_out.at[mine], delta_out.at[mine], to)

    for h in range(PARTS):
        send(("z", h), slot(h, 0, 0, 0), slot(h, 1, 0, 0), over_z)
        gather_own(h, 0)

    @pl.loop(0, 32)
    def _(n):
        t, s, q = n // 16, (n // 4) % 4, n % 4
        plane = (z + t) % 2
        yy = (y + s * (1 - plane) + q * plane) % 4
        xx = (x + q * (1 - plane) + s * plane) % 4
        chip = plane * 16 + yy * 4 + xx
        here = pl.ds(pl.multiple_of(n * ROWS, ROWS), ROWS)
        mine = pl.ds(pl.multiple_of((2 * chip + c) * ROWS, ROWS), ROWS)
        other = pl.ds(pl.multiple_of((2 * chip + 1 - c) * ROWS, ROWS), ROWS)
        pltpu.make_async_copy(hidden.at[:, mine], hid.at[pl.ds(0, TOK), here], hid_sem.at[0]).start()
        pltpu.make_async_remote_copy(
            src_ref=hidden.at[:, other],
            dst_ref=hid.at[pl.ds(TOK, TOK), here],
            send_sem=hid_sem.at[1],
            recv_sem=hid_sem.at[2],
            device_id=sibling,
            device_id_type=MESH,
        ).start()

    def hidden_wait():
        mine, theirs = hid.at[pl.ds(0, TOK)], hid.at[pl.ds(TOK, TOK)]
        pltpu.make_async_copy(mine, mine, hid_sem.at[0]).wait()
        pltpu.make_async_copy(mine, mine, hid_sem.at[1]).wait()
        pltpu.make_async_copy(theirs, theirs, hid_sem.at[2]).wait()

    def step1(h):
        gather_next(h, 0)
        gather_own(h, 1)
        gather_pass(h, 0, 0)

    def step2(h):
        gather_far(h, 0)
        gather_next(h, 1)
        gather_pass(h, 0, 3)
        gather_pass(h, 0, 1)
        gather_pass(h, 1, 0)

    def step3(h):
        gather_far(h, 1)
        gather_pass(h, 0, 2)
        gather_pass(h, 1, 3)
        gather_pass(h, 1, 1)
        gather_pass(h, 1, 2)

    def step4(h):
        for t in range(2):
            keys_add(h, t, 0)
            keys_add(h, t, 1)
            keys_add(h, t, 3)
        for t in range(2):
            keys_add(h, t, 2)
        keys_swap(h)

    step1(0)
    step2(0)
    step1(1)
    step3(0)
    hidden_wait()
    step2(1)
    step4(0)
    replicas_start()
    step3(1)
    deltas(0)
    arrived("delta", 0)
    scatter_far(0, 0)
    scatter_far(0, 1)
    step4(1)
    scatter_near(0, 0)
    scatter_near(0, 1)
    deltas(1)
    scatter_own(0, 0)
    first_far(0, 0)
    arrived("delta", 1)
    scatter_far(1, 0)
    scatter_far(1, 1)
    scatter_own(0, 1)
    first_far(0, 1)
    first_near(0, 0)
    scatter_near(1, 0)
    first_near(0, 1)
    scatter_near(1, 1)
    replicas_sum()
    first_own(0, 1)
    first_own(0, 0)
    scatter_own(1, 1)
    first_far(1, 1)
    scatter_own(1, 0)
    first_far(1, 0)
    first_near(1, 1)
    first_near(1, 0)
    finish(0)
    first_own(1, 1)
    first_own(1, 0)
    for k in (1, 2, 3):
        arrived("rep out", k)
    finish(1)
    for copy in sent.values():
        copy.wait_send()


def project(hidden, master, key_grad, diff):
    vmem = pl.BlockSpec(memory_space=pltpu.VMEM)
    f32, bf16 = jnp.float32, jnp.bfloat16
    return pl.pallas_call(
        kernel,
        out_shape=(
            jax.ShapeDtypeStruct((PARTS * WIDE, ROWS), f32),
            jax.ShapeDtypeStruct(diff.shape, f32),
        ),
        in_specs=[pl.BlockSpec(memory_space=pl.ANY), vmem, vmem, vmem],
        out_specs=(vmem, vmem),
        scratch_shapes=[
            pltpu.VMEM((2 * TOK, 32 * ROWS), bf16),
            pltpu.VMEM((PARTS, 32, ROWS, WIDE), bf16),
            pltpu.VMEM((PARTS, 2 * TOK, WIDE), f32),
            pltpu.VMEM((PARTS, TOK, WIDE), f32),
            pltpu.VMEM((PARTS, WIDE, 2 * TOK), bf16),
            pltpu.VMEM((PARTS, 2, 4, WIDE, 4 * ROWS), bf16),
            pltpu.VMEM((PARTS, 2, 4, WIDE, 4 * ROWS), bf16),
            pltpu.VMEM((PARTS, 2, WIDE, 4 * ROWS), f32),
            pltpu.VMEM((PARTS, WIDE, ROWS), f32),
            pltpu.VMEM((PARTS, WIDE, ROWS), f32),
            pltpu.VMEM((PARTS, WIDE, ROWS), f32),
            pltpu.VMEM((3, 256, 128), f32),
            pltpu.SemaphoreType.DMA((MESSAGES,)),
            pltpu.SemaphoreType.DMA((MESSAGES,)),
            pltpu.SemaphoreType.DMA((3,)),
        ],
        compiler_params=pltpu.CompilerParams(
            collective_id=0, has_side_effects=True, vmem_limit_bytes=56 * 2**20
        ),
        name="project",
    )(hidden, master, key_grad, diff)


def shards(
    hidden,
    master,
    moment_first,
    moment_second,
    key_grad,
    frag_global,
    frag_local,
    frag_moment,
    frag_index,
):
    weights = master[0]
    chosen = frag_index[0]
    glob = lax.dynamic_index_in_dim(frag_global, chosen, 0, keepdims=False)
    moment = lax.dynamic_index_in_dim(frag_moment, chosen, 0, keepdims=False)
    local = lax.dynamic_index_in_dim(frag_local[0], chosen, 0, keepdims=False)
    grad_t, delta = project(hidden[0], weights, key_grad[0], (glob - local).reshape(-1, 128))
    weights_new, first_new, second_new = adamw(weights, moment_first[0], moment_second[0], grad_t.T)
    delta = delta.reshape(-1)
    outer_moment = 0.9 * moment + delta
    outer_global = glob - 0.7 * (0.9 * outer_moment + delta)
    mixed_local = 0.5 * local + 0.5 * outer_global
    return (
        weights_new[None],
        first_new[None],
        second_new[None],
        outer_global,
        outer_moment,
        mixed_local[None],
    )


def solution(mesh):
    placed = (
        P("replica", "fsdp", None),
        P("replica", "fsdp", None),
        P("replica", "fsdp", None),
        P("replica", "fsdp", None),
        P("replica", "fsdp", None),
        P(None, "fsdp"),
        P("replica", None, "fsdp"),
        P(None, "fsdp"),
        P(),
    )
    return jax.shard_map(
        shards,
        mesh=mesh,
        in_specs=placed,
        out_specs=(
            P("replica", "fsdp", None),
            P("replica", "fsdp", None),
            P("replica", "fsdp", None),
            P("fsdp"),
            P("fsdp"),
            P("replica", "fsdp"),
        ),
        check_vma=False,
    )
```

```python
import jax
import jax.numpy as jnp
from jax import lax
from jax.experimental import pallas as pl
from jax.experimental.pallas import tpu as pltpu
from jax.sharding import PartitionSpec as P

MESH = pl.DeviceIdType.MESH
HEAD = 128
PARTS = 2
WIDE = 256
TOK = 384
ROWS = 128
PAIR = 2 * ROWS
QUARTER = 256
MESSAGES = 256

ORDER = (
    ('zsend', 0),
    ('own', 0, 0),
    ('hids',),
    ('own', 1, 0),
    ('zsend', 1),
    ('own', 0, 1),
    ('passp', 0, 0, 0),
    ('passm', 0, 0, 0),
    ('nextm', 0, 0),
    ('rep',),
    ('passp', 1, 0, 0),
    ('passm', 1, 0, 0),
    ('nextp', 0, 0),
    ('passm', 0, 1, 0),
    ('passp', 0, 1, 0),
    ('hid',),
    ('nextp', 0, 1),
    ('nextm', 0, 1),
    ('passp', 0, 0, 1),
    ('passm', 0, 0, 1),
    ('far', 0, 0),
    ('keys', 0, 0, 0),
    ('own', 1, 1),
    ('passp', 0, 1, 3),
    ('passm', 0, 1, 3),
    ('far', 0, 1),
    ('keys', 0, 1, 0),
    ('passm', 0, 0, 3),
    ('passp', 0, 0, 3),
    ('passp', 0, 1, 1),
    ('passm', 0, 1, 1),
    ('passp', 0, 0, 2),
    ('passm', 0, 0, 2),
    ('keys', 0, 0, 1),
    ('keys', 0, 0, 3),
    ('passp', 1, 1, 0),
    ('passm', 1, 1, 0),
    ('nextp', 1, 0),
    ('nextm', 1, 0),
    ('rep2',),
    ('passp', 0, 1, 2),
    ('passm', 0, 1, 2),
    ('keys', 0, 1, 1),
    ('nextm', 1, 1),
    ('keys', 0, 1, 3),
    ('keys', 0, 0, 2),
    ('nextp', 1, 1),
    ('passp', 1, 0, 3),
    ('passm', 1, 0, 3),
    ('far', 1, 0),
    ('keys', 1, 0, 0),
    ('keys', 0, 1, 2),
    ('swap', 0),
    ('passp', 1, 0, 1),
    ('passm', 1, 0, 1),
    ('far', 1, 1),
    ('keys', 1, 1, 0),
    ('passp', 1, 1, 1),
    ('passm', 1, 1, 1),
    ('deltas', 0),
    ('passp', 1, 1, 3),
    ('passm', 1, 1, 3),
    ('passp', 1, 0, 2),
    ('keys', 1, 0, 3),
    ('passm', 1, 0, 2),
    ('keys', 1, 0, 1),
    ('rfar', 0, 1, 0),
    ('rfar', 0, 0, 0),
    ('passp', 1, 1, 2),
    ('passm', 1, 1, 2),
    ('keys', 1, 1, 1),
    ('keys', 1, 1, 3),
    ('rfar', 0, 1, 1),
    ('rfar', 0, 0, 1),
    ('row0', 0, 0, 0),
    ('row0', 0, 0, 1),
    ('keys', 1, 0, 2),
    ('rn1', 0, 1, 0),
    ('rn1', 0, 0, 0),
    ('rn3', 0, 1, 0),
    ('rn3', 0, 0, 0),
    ('rn1', 0, 0, 1),
    ('rn1b', 0, 1, 0),
    ('rn3b', 0, 0, 0),
    ('keys', 1, 1, 2),
    ('swap', 1),
    ('rn3b', 0, 1, 0),
    ('row0', 0, 1, 0),
    ('row0', 0, 1, 1),
    ('rn1b', 0, 0, 0),
    ('rn1', 0, 1, 1),
    ('rn3', 0, 1, 1),
    ('rn3', 0, 0, 1),
    ('deltas', 1),
    ('rn1b', 0, 1, 1),
    ('rn3b', 0, 0, 1),
    ('rn3b', 0, 1, 1),
    ('rn1b', 0, 0, 1),
    ('repf',),
    ('rfar', 1, 1, 0),
    ('rfar', 1, 0, 0),
    ('row', 0, 1, 0),
    ('row0', 1, 0, 0),
    ('row0', 1, 0, 1),
    ('row', 0, 0, 0),
    ('cn1', 0, 1),
    ('rfar', 1, 1, 1),
    ('rfar', 1, 0, 1),
    ('row0', 1, 1, 0),
    ('row0', 1, 1, 1),
    ('rn1', 1, 1, 0),
    ('rn3', 1, 1, 0),
    ('row', 0, 0, 1),
    ('row', 0, 1, 1),
    ('cfar', 0, 1),
    ('cn3', 0, 1),
    ('rn1', 1, 0, 0),
    ('rn1', 1, 1, 1),
    ('rn3', 1, 1, 1),
    ('rn3', 1, 0, 0),
    ('rn1', 1, 0, 1),
    ('rn1b', 1, 1, 0),
    ('rn3b', 1, 1, 0),
    ('rn3', 1, 0, 1),
    ('rn1b', 1, 0, 0),
    ('rn1b', 1, 1, 1),
    ('rn3b', 1, 1, 1),
    ('cn3b', 0, 1),
    ('rn3b', 1, 0, 0),
    ('cn1b', 0, 1),
    ('cn1', 0, 0),
    ('cn3', 0, 0),
    ('rn1b', 1, 0, 1),
    ('cfar', 0, 0),
    ('rn3b', 1, 0, 1),
    ('row', 1, 1, 0),
    ('cn1', 1, 1),
    ('row', 1, 1, 1),
    ('cfar', 1, 1),
    ('cn3', 1, 1),
    ('cown', 0, 1),
    ('row', 1, 0, 0),
    ('cn1', 1, 0),
    ('cn1b', 0, 0),
    ('cn3b', 0, 0),
    ('row', 1, 0, 1),
    ('cfar', 1, 0),
    ('cn3', 1, 0),
    ('cn3b', 1, 1),
    ('cn1b', 1, 1),
    ('cown', 0, 0),
    ('cn1b', 1, 0),
    ('cn3b', 1, 0),
    ('finish', 0),
    ('cown', 1, 1),
    ('cown', 1, 0),
    ('finish', 1),
)


def norm_backward(keys, upstream):
    inverse = lax.rsqrt(jnp.mean(keys * keys, axis=-1, keepdims=True) + 1e-06)
    normed = keys * inverse
    return inverse * (upstream - normed * jnp.mean(upstream * normed, axis=-1, keepdims=True))


def kernel(
    index,
    hidden,
    master_hbm,
    key_grad_hbm,
    glob_hbm,
    local_hbm,
    moment_hbm,
    grad_out,
    global_out,
    moment_out,
    mixed_out,
    hid,
    master,
    key_grad,
    wts,
    acc,
    acc_in,
    dlt,
    gbuf,
    stage,
    stage_in,
    z_stage,
    z_in,
    final,
    frags,
    diff,
    local,
    rep_in,
    delta,
    outer,
    send_sem,
    recv_sem,
    hid_sem,
    in_sem,
    out_sem,
):
    r = lax.axis_index("replica")
    f = lax.axis_index("fsdp")
    z, y, x, c = f // 32, (f // 8) % 4, (f // 2) % 4, f % 2

    def at(zz, yy, xx, cc):
        return (r, zz * 32 + (yy % 4) * 8 + (xx % 4) * 2 + cc)

    a_up, a_down = at(z, y + z, x + 1 - z, c), at(z, y + 4 - z, x + 3 + z, c)
    b_up, b_down = at(z, y + 1 - z, x + z, c), at(z, y + 3 + z, x + 4 - z, c)
    over_z, sibling = at(1 - z, y, x, c), at(z, y, x, 1 - c)
    reps = [((r + k) % 4, f) for k in (1, 2, 3)]
    ways = (((a_up, a_down), (b_up, b_down)), ((b_up, b_down), (a_up, a_down)))

    loads = [
        pltpu.make_async_copy(src, dst, in_sem.at[n])
        for n, (src, dst) in enumerate(
            (
                (master_hbm, master),
                (key_grad_hbm, key_grad),
                (glob_hbm, frags.at[0]),
                (local_hbm, frags.at[1]),
                (moment_hbm, frags.at[2]),
            )
        )
    ]
    loads[0].start()
    barrier = pltpu.get_barrier_semaphore()
    peers = [a_up, a_down, b_up, b_down, over_z, sibling, *reps]
    for peer in peers:
        pl.semaphore_signal(barrier, inc=1, device_id=peer, device_id_type=MESH)

    def chip_of(n):
        t, s, q = n // 16, (n // 4) % 4, n % 4
        plane = (z + t) % 2
        yy = (y + s * (1 - plane) + q * plane) % 4
        xx = (x + q * (1 - plane) + s * plane) % 4
        return plane * 16 + yy * 4 + xx

    def columns(block):
        return pl.ds(pl.multiple_of(block * ROWS, ROWS), ROWS)

    @pl.loop(0, 32)
    def _(n):
        pltpu.make_async_copy(
            hidden.at[:, columns(2 * chip_of(n) + c)], hid.at[pl.ds(0, TOK), columns(n)], hid_sem.at[0]
        ).start()

    for load in loads[1:]:
        load.start()
    loads[0].wait()
    wts[0, 0] = master[:, :WIDE].astype(jnp.bfloat16)
    wts[1, 0] = master[:, WIDE:].astype(jnp.bfloat16)
    pl.semaphore_wait(barrier, len(peers))

    sent = {}

    def send(name, src, dst, to):
        n = len(sent)
        copy = pltpu.make_async_remote_copy(
            src_ref=src,
            dst_ref=dst,
            send_sem=send_sem.at[n],
            recv_sem=recv_sem.at[n],
            device_id=to,
            device_id_type=MESH,
        )
        copy.start()
        sent[name] = copy

    def arrived(*name):
        sent[name].wait_recv()

    def slot(h, t, s, q):
        return wts.at[h, 16 * t + 4 * s + q]

    lower, upper = pl.ds(0, ROWS // 2), pl.ds(ROWS // 2, ROWS // 2)

    def zsend(h):
        send(("z", h), slot(h, 0, 0, 0), slot(h, 1, 0, 0), over_z)

    def over_second(h, t, q):
        _, (up, down) = ways[t]
        src = slot(h, t, 0, q)
        send(("s+", h, t, q), src, slot(h, t, 3, q), up)
        send(("s-", h, t, q), src, slot(h, t, 1, q), down)

    def own(h, t):
        (up, down), _ = ways[t]
        if t == 1:
            arrived("z", h)
        src = slot(h, t, 0, 0)
        send(("f+", h, t), src, slot(h, t, 0, 3), up)
        send(("f-", h, t), src, slot(h, t, 0, 1), down)
        over_second(h, t, 0)

    def nextp(h, t):
        arrived("f+", h, t)
        send(("ff+", h, t), slot(h, t, 0, 3).at[lower], slot(h, t, 0, 2).at[lower], ways[t][0][0])
        over_second(h, t, 3)

    def nextm(h, t):
        arrived("f-", h, t)
        send(("ff-", h, t), slot(h, t, 0, 1).at[upper], slot(h, t, 0, 2).at[upper], ways[t][0][1])
        over_second(h, t, 1)

    def far(h, t):
        arrived("ff+", h, t)
        arrived("ff-", h, t)
        over_second(h, t, 2)

    def passp(h, t, q):
        arrived("s+", h, t, q)
        send(("ss+", h, t, q), slot(h, t, 3, q).at[lower], slot(h, t, 2, q).at[lower], ways[t][1][0])

    def passm(h, t, q):
        arrived("s-", h, t, q)
        send(("ss-", h, t, q), slot(h, t, 1, q).at[upper], slot(h, t, 2, q).at[upper], ways[t][1][1])

    summed = set()

    def keys(h, t, s):
        if s == 2:
            for q in range(4):
                arrived("ss+", h, t, q)
                arrived("ss-", h, t, q)
        first = 16 * t + 4 * s
        part = jnp.dot(
            hid[:, first * ROWS : (first + 4) * ROWS],
            wts[h, first : first + 4].reshape(4 * ROWS, WIDE),
            preferred_element_type=jnp.float32,
        )
        if h in summed:
            acc[h] += part
        else:
            acc[h] = part
        summed.add(h)

    def swap(h):
        send(("keys", h), acc.at[h, pl.ds(TOK, TOK)], acc_in.at[h], sibling)

    def deltas(h):
        if h == 0:
            loads[1].wait()
        arrived("keys", h)
        for n in range(WIDE // HEAD):
            cols = slice(n * HEAD, (n + 1) * HEAD)
            of_head = acc[h, :TOK, cols] + acc_in[h, :, cols]
            at_col = h * WIDE + n * HEAD
            up = key_grad[:, at_col : at_col + HEAD].astype(jnp.float32)
            dlt[h, n * HEAD : (n + 1) * HEAD, :TOK] = norm_backward(of_head, up).T.astype(jnp.bfloat16)
        send(("delta", h), dlt.at[h, :, pl.ds(0, TOK)], dlt.at[h, :, pl.ds(TOK, TOK)], sibling)

    low, high, both = slice(0, WIDE // 2), slice(WIDE // 2, WIDE), slice(0, WIDE)
    swapped = set()

    def part_of(k):
        return slice(k * PAIR, (k + 1) * PAIR)

    def grad_row(h, t, s, k):
        if h not in swapped:
            arrived("delta", h)
            swapped.add(h)
        first = (16 * t + 4 * s + 2 * k) * ROWS
        return jnp.dot(dlt[h], hid[:, first : first + PAIR], preferred_element_type=jnp.float32)

    def row_send(name, h, t, s, k, rows, to):
        where = (h, t, s, pl.ds(rows.start, WIDE // 2), pl.ds(k * PAIR, PAIR))
        send((name, h, t, k), stage.at[where], stage_in.at[where], to)

    def one_send(name, h, t, q, rows, to):
        where = (h, t, 0, pl.ds(rows.start, WIDE // 2), pl.ds(q * ROWS, ROWS))
        send((name, h, t), stage.at[where], stage_in.at[where], to)

    def staged(h, t, s, rows, cols, value):
        stage[h, t, s, rows, cols] = value.astype(jnp.bfloat16)

    def received(h, t, s, rows, cols):
        return stage_in[h, t, s, rows, cols].astype(jnp.float32)

    def rfar(h, t, k):
        staged(h, t, 2, both, part_of(k), grad_row(h, t, 2, k))
        row_send("rf+", h, t, 2, k, low, ways[t][1][0])
        row_send("rf-", h, t, 2, k, high, ways[t][1][1])

    def rn1(h, t, k):
        cols = part_of(k)
        value = grad_row(h, t, 1, k)
        gbuf[h, t, 1, low, cols] = value[low]
        staged(h, t, 1, high, cols, value[high])
        row_send("r+h", h, t, 1, k, high, ways[t][1][0])

    def rn3(h, t, k):
        cols = part_of(k)
        value = grad_row(h, t, 3, k)
        gbuf[h, t, 3, high, cols] = value[high]
        staged(h, t, 3, low, cols, value[low])
        row_send("r-l", h, t, 3, k, low, ways[t][1][1])

    def rn1b(h, t, k):
        cols = part_of(k)
        arrived("rf+", h, t, k)
        staged(h, t, 1, low, cols, gbuf[h, t, 1, low, cols] + received(h, t, 2, low, cols))
        row_send("r+l", h, t, 1, k, low, ways[t][1][0])

    def rn3b(h, t, k):
        cols = part_of(k)
        arrived("rf-", h, t, k)
        staged(h, t, 3, high, cols, gbuf[h, t, 3, high, cols] + received(h, t, 2, high, cols))
        row_send("r-h", h, t, 3, k, high, ways[t][1][1])

    def row0(h, t, k):
        gbuf[h, t, 0, :, part_of(k)] = grad_row(h, t, 0, k)

    def row(h, t, k):
        for name in ("r+h", "r-l", "r+l", "r-h"):
            arrived(name, h, t, k)
        cols = part_of(k)
        gbuf[h, t, 0, :, cols] += received(h, t, 1, both, cols) + received(h, t, 3, both, cols)

    def cols_of(q):
        return slice(q * ROWS, (q + 1) * ROWS)

    def cfar(h, t):
        staged(h, t, 0, both, cols_of(2), gbuf[h, t, 0, :, cols_of(2)])
        one_send("cf+", h, t, 2, low, ways[t][0][0])
        one_send("cf-", h, t, 2, high, ways[t][0][1])

    def cn1(h, t):
        staged(h, t, 0, high, cols_of(1), gbuf[h, t, 0, high, cols_of(1)])
        one_send("c+h", h, t, 1, high, ways[t][0][0])

    def cn3(h, t):
        staged(h, t, 0, low, cols_of(3), gbuf[h, t, 0, low, cols_of(3)])
        one_send("c-l", h, t, 3, low, ways[t][0][1])

    def cn1b(h, t):
        arrived("cf+", h, t)
        staged(h, t, 0, low, cols_of(1), gbuf[h, t, 0, low, cols_of(1)] + received(h, t, 0, low, cols_of(2)))
        one_send("c+l", h, t, 1, low, ways[t][0][0])

    def cn3b(h, t):
        arrived("cf-", h, t)
        staged(h, t, 0, high, cols_of(3), gbuf[h, t, 0, high, cols_of(3)] + received(h, t, 0, high, cols_of(2)))
        one_send("c-h", h, t, 3, high, ways[t][0][1])

    def cown(h, t):
        for name in ("c+h", "c-l", "c+l", "c-h"):
            arrived(name, h, t)
        total = gbuf[h, t, 0, :, cols_of(0)] + received(h, t, 0, both, cols_of(1)) + received(h, t, 0, both, cols_of(3))
        if t == 1:
            z_stage[h] = total
            send(("gz", h), z_stage.at[h], z_in.at[h], over_z)
        else:
            final[h] = total

    def finish(h):
        arrived("gz", h)
        grad_out[:, h * WIDE : (h + 1) * WIDE] = (final[h] + z_in[h]).T

    def hids():
        @pl.loop(0, 32)
        def _(n):
            pltpu.make_async_remote_copy(
                src_ref=hidden.at[:, columns(2 * chip_of(n) + 1 - c)],
                dst_ref=hid.at[pl.ds(TOK, TOK), columns(n)],
                send_sem=hid_sem.at[1],
                recv_sem=hid_sem.at[2],
                device_id=sibling,
                device_id_type=MESH,
            ).start()

    mine, theirs = hid.at[pl.ds(0, TOK)], hid.at[pl.ds(TOK, TOK)]

    def hid_wait():
        pltpu.make_async_copy(mine, mine, hid_sem.at[0]).wait()
        pltpu.make_async_copy(theirs, theirs, hid_sem.at[2]).wait()

    def chosen(n, rows):
        first = frags[n, pl.ds(2 * rows.start, rows.size, stride=2), :]
        second = frags[n, pl.ds(2 * rows.start + 1, rows.size, stride=2), :]
        return jnp.where(index[0] == 0, first, second)

    def rep():
        loads[2].wait()
        loads[3].wait()
        for n in range(4):
            rows = pl.ds(n * QUARTER, QUARTER)
            own_local = chosen(1, rows)
            local[rows, :] = own_local
            diff[rows, :] = chosen(0, rows) - own_local
        for k, to in zip((1, 2, 3), reps):
            send(("rep", k), diff.at[pl.ds(((r + k) % 4) * QUARTER, QUARTER)], rep_in.at[k - 1], to)

    def rep2():
        for k in (1, 2, 3):
            arrived("rep", k)
        own_rows = pl.ds(r * QUARTER, QUARTER)
        delta[own_rows, :] = (diff[own_rows, :] + rep_in[0] + rep_in[1] + rep_in[2]) * 0.25
        for k, to in zip((1, 2, 3), reps):
            send(("rep out", k), delta.at[own_rows], delta.at[own_rows], to)

    stores = [
        pltpu.make_async_copy(outer.at[n], dst, out_sem.at[n])
        for n, dst in enumerate((global_out, moment_out, mixed_out))
    ]

    def repf():
        loads[4].wait()
        for k in (1, 2, 3):
            arrived("rep out", k)
        for n in range(4):
            rows = pl.ds(n * QUARTER, QUARTER)
            step = delta[rows, :]
            outer_moment = 0.9 * chosen(2, rows) + step
            outer_global = chosen(0, rows) - 0.7 * (0.9 * outer_moment + step)
            outer[0, rows, :] = outer_global
            outer[1, rows, :] = outer_moment
            outer[2, rows, :] = 0.5 * local[rows, :] + 0.5 * outer_global
        for store in stores:
            store.start()

    steps = dict(
        zsend=zsend, own=own, nextp=nextp, nextm=nextm, far=far, passp=passp, passm=passm, keys=keys, swap=swap,
        deltas=deltas, rfar=rfar, rn1=rn1, rn3=rn3, rn1b=rn1b, rn3b=rn3b, row0=row0, row=row, cfar=cfar, cn1=cn1,
        cn3=cn3, cn1b=cn1b, cn3b=cn3b, cown=cown, finish=finish, hids=hids, hid=hid_wait, rep=rep, rep2=rep2, repf=repf,
    )
    for name, *where in ORDER:
        steps[name](*where)
    for copy in sent.values():
        copy.wait_send()
    pltpu.make_async_copy(mine, mine, hid_sem.at[1]).wait()
    for store in stores:
        store.wait()


def project(index, hidden, master, key_grad, glob, local, moment):
    vmem, anywhere = pl.BlockSpec(memory_space=pltpu.VMEM), pl.BlockSpec(memory_space=pl.ANY)
    f32, bf16 = jnp.float32, jnp.bfloat16
    part = (4 * QUARTER, 128)
    row = (PARTS, 2, 4, WIDE, 4 * ROWS)
    return pl.pallas_call(
        kernel,
        out_shape=(
            jax.ShapeDtypeStruct((ROWS, PARTS * WIDE), f32),
            *[jax.ShapeDtypeStruct(part, f32)] * 3,
        ),
        in_specs=[pl.BlockSpec(memory_space=pltpu.SMEM), *[anywhere] * 6],
        out_specs=(vmem, *[anywhere] * 3),
        scratch_shapes=[
            pltpu.VMEM((2 * TOK, 32 * ROWS), bf16),
            pltpu.VMEM((ROWS, PARTS * WIDE), f32),
            pltpu.VMEM((TOK, PARTS * WIDE), bf16),
            pltpu.VMEM((PARTS, 32, ROWS, WIDE), bf16),
            pltpu.VMEM((PARTS, 2 * TOK, WIDE), f32),
            pltpu.VMEM((PARTS, TOK, WIDE), f32),
            pltpu.VMEM((PARTS, WIDE, 2 * TOK), bf16),
            pltpu.VMEM(row, f32),
            pltpu.VMEM(row, bf16),
            pltpu.VMEM(row, bf16),
            pltpu.VMEM((PARTS, WIDE, ROWS), f32),
            pltpu.VMEM((PARTS, WIDE, ROWS), f32),
            pltpu.VMEM((PARTS, WIDE, ROWS), f32),
            pltpu.VMEM((3, 8 * QUARTER, 128), f32),
            pltpu.VMEM(part, f32),
            pltpu.VMEM(part, f32),
            pltpu.VMEM((3, QUARTER, 128), f32),
            pltpu.VMEM(part, f32),
            pltpu.VMEM((3, *part), f32),
            pltpu.SemaphoreType.DMA((MESSAGES,)),
            pltpu.SemaphoreType.DMA((MESSAGES,)),
            pltpu.SemaphoreType.DMA((3,)),
            pltpu.SemaphoreType.DMA((5,)),
            pltpu.SemaphoreType.DMA((3,)),
        ],
        compiler_params=pltpu.CompilerParams(
            collective_id=0, has_side_effects=True, vmem_limit_bytes=56 * 2**20
        ),
        name="project",
    )(index, hidden, master, key_grad, glob, local, moment)


def last_kernel(*refs):
    ins, outs, states, outer, in_sem, out_sem = refs[:7], refs[7:13], *refs[13:]
    held = [states.at[n] for n in range(4)] + [outer.at[n] for n in range(3)]
    results = [states.at[n] for n in range(4, 7)] + [outer.at[n] for n in range(3)]
    loads = [pltpu.make_async_copy(src, dst, in_sem.at[n]) for n, (src, dst) in enumerate(zip(ins, held))]
    stores = [pltpu.make_async_copy(src, dst, out_sem.at[n]) for n, (src, dst) in enumerate(zip(results, outs))]
    for load in loads:
        load.start()
    for load in loads[:4]:
        load.wait()
    gradient, weights = states[0], states[1]
    first_new = 0.9 * states[2] + 0.1 * gradient
    second_new = 0.95 * states[3] + 0.05 * gradient * gradient
    first_hat = first_new / (1.0 - 0.9**10)
    second_hat = second_new / (1.0 - 0.95**10)
    states[4] = weights - 0.01 * (first_hat / (jnp.sqrt(second_hat) + 1e-08) + 0.1 * weights)
    states[5] = first_new
    states[6] = second_new
    for store in stores[:3]:
        store.start()
    for load, store in zip(loads[4:], stores[3:]):
        load.wait()
        store.start()
    for store in stores:
        store.wait()


def last(grad, master, first, second, *outer):
    anywhere = pl.BlockSpec(memory_space=pl.ANY)
    return pl.pallas_call(
        last_kernel,
        out_shape=tuple(jax.ShapeDtypeStruct(v.shape, jnp.float32) for v in (master, first, second, *outer)),
        in_specs=[anywhere] * 7,
        out_specs=(anywhere,) * 6,
        scratch_shapes=[
            pltpu.VMEM((7, *master.shape), jnp.float32),
            pltpu.VMEM((3, *outer[0].shape), jnp.float32),
            pltpu.SemaphoreType.DMA((7,)),
            pltpu.SemaphoreType.DMA((6,)),
        ],
        compiler_params=pltpu.CompilerParams(vmem_limit_bytes=56 * 2**20),
        name="last",
    )(grad, master, first, second, *outer)


def rows_of(fragments):
    return fragments.reshape(2, -1, 128).transpose(1, 0, 2).reshape(-1, 128)


def shards(
    hidden,
    master,
    moment_first,
    moment_second,
    key_grad,
    frag_global,
    frag_local,
    frag_moment,
    frag_index,
):
    grad, *outer = project(
        frag_index,
        hidden[0],
        master[0],
        key_grad[0],
        rows_of(frag_global),
        rows_of(frag_local[0]),
        rows_of(frag_moment),
    )
    weights_new, first_new, second_new, *outer = last(grad, master[0], moment_first[0], moment_second[0], *outer)
    outer_global, outer_moment, mixed_local = (part.reshape(-1) for part in outer)
    return (
        weights_new[None],
        first_new[None],
        second_new[None],
        outer_global,
        outer_moment,
        mixed_local[None],
    )


def solution(mesh):
    placed = (
        P("replica", "fsdp", None),
        P("replica", "fsdp", None),
        P("replica", "fsdp", None),
        P("replica", "fsdp", None),
        P("replica", "fsdp", None),
        P(None, "fsdp"),
        P("replica", None, "fsdp"),
        P(None, "fsdp"),
        P(),
    )
    return jax.shard_map(
        shards,
        mesh=mesh,
        in_specs=placed,
        out_specs=(
            P("replica", "fsdp", None),
            P("replica", "fsdp", None),
            P("replica", "fsdp", None),
            P("fsdp"),
            P("fsdp"),
            P("replica", "fsdp"),
        ),
        check_vma=False,
    )
```

```python
import jax
import jax.numpy as jnp
from jax import lax
from jax.experimental import pallas as pl
from jax.experimental.pallas import tpu as pltpu
from jax.sharding import PartitionSpec as P

MESH = pl.DeviceIdType.MESH
HEAD = 128
PARTS = 2
WIDE = 256
TOK = 384
ROWS = 128
SLOTS = 1
QUARTER = 256
ARRIVALS = 120

ORDER = (
    ('zsend', 0),
    ('own', 1, 0),
    ('hids',),
    ('zsend', 1),
    ('own', 0, 0),
    ('own', 0, 1),
    ('passp', 1, 0, 0),
    ('passm', 1, 0, 0),
    ('nextm', 1, 0),
    ('rep',),
    ('passm', 0, 0, 0),
    ('passp', 0, 0, 0),
    ('nextp', 0, 0),
    ('nextm', 0, 0),
    ('passp', 0, 1, 0),
    ('passm', 0, 1, 0),
    ('hid',),
    ('kgt',),
    ('nextm', 0, 1),
    ('nextp', 0, 1),
    ('passm', 0, 0, 3),
    ('passp', 0, 0, 3),
    ('far', 0, 0),
    ('passp', 1, 0, 1),
    ('passm', 1, 0, 1),
    ('own', 1, 1),
    ('passp', 0, 1, 1),
    ('passm', 0, 1, 1),
    ('passm', 0, 0, 1),
    ('passp', 0, 0, 1),
    ('far', 0, 1),
    ('keys', 0, 0),
    ('passp', 0, 1, 3),
    ('passm', 0, 1, 3),
    ('passm', 0, 0, 2),
    ('passp', 0, 0, 2),
    ('keys', 0, 1),
    ('nextp', 1, 0),
    ('passm', 1, 1, 0),
    ('passp', 1, 1, 0),
    ('nextp', 1, 1),
    ('nextm', 1, 1),
    ('keys', 0, 3),
    ('passm', 0, 1, 2),
    ('passp', 0, 1, 2),
    ('keys', 0, 2),
    ('far', 1, 0),
    ('passp', 1, 0, 3),
    ('passm', 1, 0, 3),
    ('passm', 1, 1, 3),
    ('passp', 1, 1, 3),
    ('far', 1, 1),
    ('keys', 1, 0),
    ('keys', 0, 4),
    ('passm', 1, 1, 1),
    ('swap', 0),
    ('passp', 1, 1, 1),
    ('rep2',),
    ('passp', 1, 0, 2),
    ('passm', 1, 0, 2),
    ('keys', 1, 1),
    ('deltas', 0),
    ('passm', 1, 1, 2),
    ('passp', 1, 1, 2),
    ('keys', 1, 2),
    ('grad', 0, 2),
    ('rfar', 0, 0, 2),
    ('rfar', 0, 1, 3),
    ('rfar', 0, 1, 1),
    ('rfar', 0, 0, 0),
    ('keys', 1, 3),
    ('rfar', 0, 1, 0),
    ('rfar', 0, 0, 3),
    ('grad', 0, 0),
    ('rfar', 0, 1, 2),
    ('rfar', 0, 0, 1),
    ('keys', 1, 4),
    ('swap', 1),
    ('grad', 0, 3),
    ('rn3', 0, 0, 3),
    ('rn3', 0, 0, 0),
    ('rn3', 0, 1, 3),
    ('rn3', 0, 1, 2),
    ('grad', 0, 1),
    ('rn1', 0, 1, 2),
    ('rn1', 0, 1, 1),
    ('rn1', 0, 0, 2),
    ('rn1b', 0, 0, 2),
    ('rn3', 0, 0, 2),
    ('rn3', 0, 1, 1),
    ('rn3b', 0, 0, 2),
    ('rn1b', 0, 1, 1),
    ('deltas', 1),
    ('rn1', 0, 0, 1),
    ('rn3b', 0, 1, 1),
    ('rn3', 0, 0, 1),
    ('rn3b', 0, 1, 3),
    ('rn1', 0, 1, 0),
    ('rn1', 0, 0, 3),
    ('rn3b', 0, 0, 3),
    ('rn1b', 0, 1, 2),
    ('rn1b', 0, 0, 3),
    ('rn3b', 0, 1, 2),
    ('grad', 1, 2),
    ('rfar', 1, 0, 1),
    ('rfar', 1, 1, 2),
    ('grad', 1, 3),
    ('rfar', 1, 1, 1),
    ('rn1', 0, 1, 3),
    ('rn1b', 0, 1, 3),
    ('rfar', 1, 1, 3),
    ('rn3', 1, 0, 1),
    ('rn3', 1, 0, 2),
    ('grad', 1, 1),
    ('row', 0, 0, 2),
    ('rn1', 1, 0, 2),
    ('row', 0, 1, 1),
    ('rn1', 1, 1, 3),
    ('rn3', 1, 1, 2),
    ('rn3', 1, 1, 3),
    ('rfar', 1, 0, 2),
    ('rn1', 1, 1, 2),
    ('rn3', 1, 0, 0),
    ('grad', 1, 0),
    ('row', 0, 0, 3),
    ('row', 0, 1, 2),
    ('rn1b', 0, 1, 0),
    ('rn3b', 1, 1, 2),
    ('rn1b', 1, 1, 2),
    ('rn3b', 1, 0, 1),
    ('rn1', 1, 0, 1),
    ('rn1', 1, 1, 1),
    ('rn3', 1, 1, 1),
    ('rn3', 1, 0, 3),
    ('rn3b', 1, 1, 1),
    ('rn1b', 1, 0, 1),
    ('rn1b', 1, 1, 1),
    ('rn3', 0, 1, 0),
    ('row', 0, 1, 3),
    ('rn3b', 1, 1, 3),
    ('rn1b', 1, 1, 3),
    ('rfar', 1, 0, 3),
    ('repf',),
    ('rn3b', 1, 0, 2),
    ('rn1b', 1, 0, 2),
    ('rn1b', 0, 0, 1),
    ('rn1', 1, 0, 0),
    ('rfar', 1, 1, 0),
    ('rn3', 1, 1, 0),
    ('rn3b', 0, 1, 0),
    ('row', 1, 1, 2),
    ('zadd', 0, 2),
    ('rn1', 0, 0, 0),
    ('rn1', 1, 0, 3),
    ('rn3b', 0, 0, 1),
    ('rn3b', 0, 0, 0),
    ('rn1b', 0, 0, 0),
    ('cfar', 0),
    ('row', 1, 0, 1),
    ('row', 1, 1, 1),
    ('rn1', 1, 1, 0),
    ('rfar', 1, 0, 0),
    ('zadd', 0, 3),
    ('cn3', 0),
    ('row', 1, 1, 3),
    ('rn1b', 1, 0, 3),
    ('rn3b', 1, 0, 3),
    ('rn3b', 1, 1, 0),
    ('row', 1, 0, 2),
    ('row', 0, 1, 0),
    ('rn1b', 1, 1, 0),
    ('zadd', 1, 2),
    ('cfar', 1),
    ('row', 0, 0, 1),
    ('zadd', 0, 1),
    ('cn1', 0),
    ('cn3b', 0),
    ('cn1b', 0),
    ('row', 0, 0, 0),
    ('rn3b', 1, 0, 0),
    ('zadd', 1, 1),
    ('cn1', 1),
    ('rn1b', 1, 0, 0),
    ('row', 1, 0, 3),
    ('zadd', 1, 3),
    ('row', 1, 1, 0),
    ('cn3', 1),
    ('cn3b', 1),
    ('cn1b', 1),
    ('zadd', 0, 0),
    ('finish', 0),
    ('row', 1, 0, 0),
    ('zadd', 1, 0),
    ('finish', 1),
)


def norm_backward(keys, upstream):
    inverse = lax.rsqrt(jnp.mean(keys * keys, axis=0, keepdims=True) + 1e-06)
    normed = keys * inverse
    return inverse * (upstream - normed * jnp.mean(upstream * normed, axis=0, keepdims=True))


def kernel(
    index,
    hidden,
    master_hbm,
    key_grad_hbm,
    glob_hbm,
    local_hbm,
    moment_hbm,
    grad_out,
    global_out,
    moment_out,
    mixed_out,
    hid,
    master,
    key_grad,
    key_grad_t,
    wts,
    acc,
    acc_in,
    dlt,
    gbuf,
    stage,
    stage_in,
    z_stage,
    z_in,
    wide,
    wide_in,
    frags,
    diff,
    local,
    rep_in,
    delta,
    outer,
    send_sem,
    recv_sem,
    hid_sem,
    in_sem,
    out_sem,
):
    r = lax.axis_index("replica")
    f = lax.axis_index("fsdp")
    z, y, x, c = f // 32, (f // 8) % 4, (f // 2) % 4, f % 2

    def at(zz, yy, xx, cc):
        return (r, zz * 32 + (yy % 4) * 8 + (xx % 4) * 2 + cc)

    a_up, a_down = at(z, y + z, x + 1 - z, c), at(z, y + 4 - z, x + 3 + z, c)
    b_up, b_down = at(z, y + 1 - z, x + z, c), at(z, y + 3 + z, x + 4 - z, c)
    over_z, sibling = at(1 - z, y, x, c), at(z, y, x, 1 - c)
    reps = [((r + k) % 4, f) for k in (1, 2, 3)]
    axes = ((a_up, a_down), (b_up, b_down))

    def ways(h, t):
        return axes if (h + t) % 2 == 0 else axes[::-1]


    loads = [
        pltpu.make_async_copy(src, dst, in_sem.at[n])
        for n, (src, dst) in enumerate(
            (
                (master_hbm, master),
                (key_grad_hbm, key_grad),
                (glob_hbm, frags.at[0]),
                (local_hbm, frags.at[1]),
                (moment_hbm, frags.at[2]),
            )
        )
    ]
    loads[0].start()
    barrier = pltpu.get_barrier_semaphore()
    peers = [a_up, a_down, b_up, b_down, over_z, sibling, *reps]
    for peer in peers:
        pl.semaphore_signal(barrier, inc=1, device_id=peer, device_id_type=MESH)

    def chip_of(n):
        t, s, q = n // 16, (n // 4) % 4, n % 4
        plane = (z + t) % 2
        yy = (y + s * (1 - plane) + q * plane) % 4
        xx = (x + q * (1 - plane) + s * plane) % 4
        return plane * 16 + yy * 4 + xx

    def columns(block):
        return pl.ds(pl.multiple_of(block * ROWS, ROWS), ROWS)

    @pl.loop(0, 32)
    def _(n):
        pltpu.make_async_copy(
            hidden.at[:, columns(2 * chip_of(n) + c)], hid.at[pl.ds(0, TOK), columns(n)], hid_sem.at[0]
        ).start()

    for load in loads[1:]:
        load.start()
    loads[0].wait()
    wts[0, 0] = master[:, :WIDE].T.astype(jnp.bfloat16)
    wts[1, 0] = master[:, WIDE:].T.astype(jnp.bfloat16)
    pl.semaphore_wait(barrier, len(peers))

    arrivals = {}

    def send(what, group, src, dst, to):
        pltpu.make_async_remote_copy(
            src_ref=src,
            dst_ref=dst,
            send_sem=send_sem.at[group],
            recv_sem=recv_sem.at[arrivals.setdefault(what, len(arrivals))],
            device_id=to,
            device_id_type=MESH,
        ).start()

    def taken(semaphore, as_large):
        pltpu.make_async_copy(as_large, as_large, semaphore).wait()

    def arrived(what, as_large):
        taken(recv_sem.at[arrivals[what]], as_large)

    gather, scatter, sums, keys_swap, delta_swap, summed, spread = range(7)

    def slot(h, t, s, q):
        return wts.at[h, 16 * t + 4 * s + q]

    lower, upper = pl.ds(0, WIDE // 2), pl.ds(WIDE // 2, WIDE // 2)

    def zsend(h):
        send(("z", h), gather, slot(h, 0, 0, 0), slot(h, 1, 0, 0), over_z)

    def over_second(h, t, q):
        _, (up, down) = ways(h, t)
        src = slot(h, t, 0, q)
        send(("s+", h, t, q), gather, src, slot(h, t, 3, q), up)
        send(("s-", h, t, q), gather, src, slot(h, t, 1, q), down)

    def own(h, t):
        (up, down), _ = ways(h, t)
        if t == 1:
            arrived(("z", h), slot(h, 1, 0, 0))
        src = slot(h, t, 0, 0)
        send(("f+", h, t), gather, src, slot(h, t, 0, 3), up)
        send(("f-", h, t), gather, src, slot(h, t, 0, 1), down)
        over_second(h, t, 0)

    def nextp(h, t):
        arrived(("f+", h, t), slot(h, t, 0, 3))
        send(("ff", h, t), gather, slot(h, t, 0, 3).at[lower], slot(h, t, 0, 2).at[lower], ways(h, t)[0][0])
        over_second(h, t, 3)

    def nextm(h, t):
        arrived(("f-", h, t), slot(h, t, 0, 1))
        send(("ff", h, t), gather, slot(h, t, 0, 1).at[upper], slot(h, t, 0, 2).at[upper], ways(h, t)[0][1])
        over_second(h, t, 1)

    def far(h, t):
        arrived(("ff", h, t), slot(h, t, 0, 2))
        over_second(h, t, 2)

    def passp(h, t, q):
        arrived(("s+", h, t, q), slot(h, t, 3, q))
        send(("ss", h, t), gather, slot(h, t, 3, q).at[lower], slot(h, t, 2, q).at[lower], ways(h, t)[1][0])

    def passm(h, t, q):
        arrived(("s-", h, t, q), slot(h, t, 1, q))
        send(("ss", h, t), gather, slot(h, t, 1, q).at[upper], slot(h, t, 2, q).at[upper], ways(h, t)[1][1])

    def hidden_of(h, rows):
        blocks = [16 * t + (4 * s + q if h == 0 else 4 * q + s) for t, s in rows for q in range(4)]
        return jnp.concatenate([hid[:, n * ROWS : (n + 1) * ROWS] for n in blocks], axis=1)

    def keys(h, n):
        rows = (((0, 0), (1, 0)), ((0, 1), (0, 3)), ((1, 1), (1, 3)), ((0, 2),), ((1, 2),))[n]
        if n >= 3:
            arrived(("ss", h, n - 3), wts.at[h, pl.ds(0, 4)])
        weights = [wts[h, 16 * t + 4 * s + q] for t, s in rows for q in range(4)]
        part = lax.dot_general(
            jnp.concatenate(weights, axis=1),
            hidden_of(h, rows),
            (((1,), (1,)), ((), ())),
            preferred_element_type=jnp.float32,
        )
        if n == 0:
            acc[h] = part
        else:
            acc[h] += part

    def swap(h):
        send(("keys", h), keys_swap, acc.at[h, :, pl.ds(TOK, TOK)], acc_in.at[h], sibling)

    def kgt():
        loads[1].wait()
        key_grad_t[...] = key_grad[...].astype(jnp.float32).T

    def deltas(h):
        arrived(("keys", h), acc_in.at[h])
        for n in range(WIDE // HEAD):
            rows, of_all = pl.ds(n * HEAD, HEAD), pl.ds(h * WIDE + n * HEAD, HEAD)
            of_head = acc[h, rows, :TOK] + acc_in[h, rows, :]
            dlt[h, rows, :TOK] = norm_backward(of_head, key_grad_t[of_all, :]).astype(jnp.bfloat16)
        send(("delta", h), delta_swap, dlt.at[h, :, pl.ds(0, TOK)], dlt.at[h, :, pl.ds(TOK, TOK)], sibling)

    low, high, both = slice(0, WIDE // 2), slice(WIDE // 2, WIDE), slice(0, WIDE)

    def grad(h, s):
        if s == 2:
            arrived(("delta", h), dlt.at[h, :, pl.ds(TOK, TOK)])
        value = jnp.dot(dlt[h], hidden_of(h, ((0, s), (1, s))), preferred_element_type=jnp.float32)
        for t in range(2):
            one = value[:, t * 4 * ROWS : (t + 1) * 4 * ROWS]
            if s == 2:
                stage[h, t, s] = one.astype(jnp.bfloat16)
            elif s == 0:
                gbuf[h, t, s] = one
            else:
                now, later = (high, low) if s == 1 else (low, high)
                stage[h, t, s, now, :] = one[now].astype(jnp.bfloat16)
                gbuf[h, t, s, later, :] = one[later]

    def cols_of(q):
        return slice(q * ROWS, (q + 1) * ROWS)

    def cols_in(k):
        return slice(k * SLOTS * ROWS, (k + 1) * SLOTS * ROWS)

    def half_of(h, t, s, k, rows):
        return (h, t, s, pl.ds(rows.start, WIDE // 2), pl.ds(k * SLOTS * ROWS, SLOTS * ROWS))

    def row_send(name, h, t, s, k, rows, to):
        where = half_of(h, t, s, k, rows)
        send((name, h, t, k), scatter, stage.at[where], stage_in.at[where], to)

    def received(h, t, s, cols, rows):
        return stage_in[h, t, s, rows, cols].astype(jnp.float32)

    def rfar(h, t, k):
        row_send("rf+", h, t, 2, k, low, ways(h, t)[1][0])
        row_send("rf-", h, t, 2, k, high, ways(h, t)[1][1])

    def rn1(h, t, k):
        row_send("r", h, t, 1, k, high, ways(h, t)[1][0])

    def rn3(h, t, k):
        row_send("r", h, t, 3, k, low, ways(h, t)[1][1])

    def rn1b(h, t, k):
        arrived(("rf+", h, t, k), stage_in.at[half_of(h, t, 2, k, low)])
        total = gbuf[h, t, 1, low, cols_in(k)] + received(h, t, 2, cols_in(k), low)
        stage[h, t, 1, low, cols_in(k)] = total.astype(jnp.bfloat16)
        row_send("r", h, t, 1, k, low, ways(h, t)[1][0])

    def rn3b(h, t, k):
        arrived(("rf-", h, t, k), stage_in.at[half_of(h, t, 2, k, high)])
        total = gbuf[h, t, 3, high, cols_in(k)] + received(h, t, 2, cols_in(k), high)
        stage[h, t, 3, high, cols_in(k)] = total.astype(jnp.bfloat16)
        row_send("r", h, t, 3, k, high, ways(h, t)[1][1])

    def row(h, t, k):
        arrived(("r", h, t, k), stage_in.at[h, t, pl.ds(0, 2), :, pl.ds(k * SLOTS * ROWS, SLOTS * ROWS)])
        cols = cols_in(k)
        total = gbuf[h, t, 0, :, cols] + received(h, t, 1, cols, both) + received(h, t, 3, cols, both)
        if t == 1:
            z_stage[h, k] = total.astype(z_stage.dtype)
            send(("zr", h, k), scatter, z_stage.at[h, k], z_in.at[h, k], over_z)
        else:
            gbuf[h, t, 0, :, cols] = total

    def zadd(h, k):
        arrived(("zr", h, k), z_in.at[h, k])
        gbuf[h, 0, 0, :, cols_in(k)] += z_in[h, k].astype(jnp.float32)

    def own_slot(h, q, rows):
        return gbuf[h, 0, 0, rows, cols_of(q)]

    def half_slot(h, q, rows):
        return (h, 0, 0, pl.ds(rows.start, WIDE // 2), pl.ds(q * ROWS, ROWS))

    def one_send(name, h, q, rows, to, value):
        stage[h, 0, 0, rows, cols_of(q)] = value.astype(jnp.bfloat16)
        where = half_slot(h, q, rows)
        send((name, h), scatter, stage.at[where], stage_in.at[where], to)

    def sum_send(h, n, to, value):
        wide[h, n] = value
        send(("sum", h), sums, wide.at[h, n], wide_in.at[h, n], to)

    def cfar(h):
        one_send("cf+", h, 2, low, ways(h, 0)[0][0], own_slot(h, 2, low))
        one_send("cf-", h, 2, high, ways(h, 0)[0][1], own_slot(h, 2, high))

    def cn1(h):
        one_send("c", h, 1, high, ways(h, 0)[0][0], own_slot(h, 1, high))

    def cn3(h):
        one_send("c", h, 3, low, ways(h, 0)[0][1], own_slot(h, 3, low))

    def cn1b(h):
        arrived(("cf+", h), stage_in.at[half_slot(h, 2, low)])
        sum_send(h, 0, ways(h, 0)[0][0], own_slot(h, 1, low) + received(h, 0, 0, cols_of(2), low))

    def cn3b(h):
        arrived(("cf-", h), stage_in.at[half_slot(h, 2, high)])
        sum_send(h, 1, ways(h, 0)[0][1], own_slot(h, 3, high) + received(h, 0, 0, cols_of(2), high))

    def finish(h):
        arrived(("c", h), stage_in.at[h, 0, 0, :, pl.ds(0, ROWS)])
        arrived(("sum", h), wide_in.at[h])
        own = own_slot(h, 0, both)
        into_low = wide_in[h, 0] + received(h, 0, 0, cols_of(3), low)
        into_high = received(h, 0, 0, cols_of(1), high) + wide_in[h, 1]
        grad_out[:, h * WIDE : h * WIDE + WIDE // 2] = (own[low] + into_low).T
        grad_out[:, h * WIDE + WIDE // 2 : (h + 1) * WIDE] = (own[high] + into_high).T

    def hids():
        @pl.loop(0, 32)
        def _(n):
            pltpu.make_async_remote_copy(
                src_ref=hidden.at[:, columns(2 * chip_of(n) + 1 - c)],
                dst_ref=hid.at[pl.ds(TOK, TOK), columns(n)],
                send_sem=hid_sem.at[1],
                recv_sem=hid_sem.at[2],
                device_id=sibling,
                device_id_type=MESH,
            ).start()

    mine, theirs = hid.at[pl.ds(0, TOK)], hid.at[pl.ds(TOK, TOK)]

    def hid_wait():
        taken(hid_sem.at[0], mine)
        taken(hid_sem.at[2], theirs)

    def chosen(n, rows):
        first = frags[n, pl.ds(2 * rows.start, rows.size, stride=2), :]
        second = frags[n, pl.ds(2 * rows.start + 1, rows.size, stride=2), :]
        return jnp.where(index[0] == 0, first, second)

    def rep():
        loads[2].wait()
        loads[3].wait()
        for n in range(4):
            rows = pl.ds(n * QUARTER, QUARTER)
            own_local = chosen(1, rows)
            local[rows, :] = own_local
            diff[rows, :] = chosen(0, rows) - own_local
        for k, to in zip((1, 2, 3), reps):
            send("rep", summed, diff.at[pl.ds(((r + k) % 4) * QUARTER, QUARTER)], rep_in.at[k - 1], to)

    def rep2():
        arrived("rep", rep_in)
        own_rows = pl.ds(r * QUARTER, QUARTER)
        delta[own_rows, :] = (diff[own_rows, :] + rep_in[0] + rep_in[1] + rep_in[2]) * 0.25
        for k, to in zip((1, 2, 3), reps):
            send("rep out", spread, delta.at[own_rows], delta.at[own_rows], to)

    stores = [
        pltpu.make_async_copy(outer.at[n], dst, out_sem.at[n])
        for n, dst in enumerate((global_out, moment_out, mixed_out))
    ]

    def repf():
        loads[4].wait()
        arrived("rep out", rep_in)
        for n in range(4):
            rows = pl.ds(n * QUARTER, QUARTER)
            step = delta[rows, :]
            outer_moment = 0.9 * chosen(2, rows) + step
            outer_global = chosen(0, rows) - 0.7 * (0.9 * outer_moment + step)
            outer[0, rows, :] = outer_global
            outer[1, rows, :] = outer_moment
            outer[2, rows, :] = 0.5 * local[rows, :] + 0.5 * outer_global
        for store in stores:
            store.start()

    steps = dict(
        zsend=zsend, own=own, nextp=nextp, nextm=nextm, far=far, passp=passp, passm=passm, keys=keys, swap=swap,
        deltas=deltas, grad=grad, rfar=rfar, rn1=rn1, rn3=rn3, rn1b=rn1b, rn3b=rn3b, row=row, zadd=zadd, cfar=cfar,
        cn1=cn1, cn3=cn3, cn1b=cn1b, cn3b=cn3b, finish=finish, hids=hids, hid=hid_wait, kgt=kgt, rep=rep, rep2=rep2, repf=repf,
    )
    for name, *where in ORDER:
        steps[name](*where)
    assert len(arrivals) == ARRIVALS
    for group, as_large in (
        (gather, wts.at[:, pl.ds(0, 31)]),
        (scatter, wts.at[:, pl.ds(0, 30)]),
        (sums, wide_in),
        (keys_swap, acc_in),
        (delta_swap, dlt.at[:, :, pl.ds(0, TOK)]),
        (summed, rep_in),
        (spread, rep_in),
    ):
        taken(send_sem.at[group], as_large)
    taken(hid_sem.at[1], mine)
    for store in stores:
        store.wait()


def project(index, hidden, master, key_grad, glob, local, moment):
    vmem, anywhere = pl.BlockSpec(memory_space=pltpu.VMEM), pl.BlockSpec(memory_space=pl.ANY)
    f32, bf16 = jnp.float32, jnp.bfloat16
    part = (4 * QUARTER, 128)
    row = (PARTS, 2, 4, WIDE, 4 * ROWS)
    return pl.pallas_call(
        kernel,
        out_shape=(
            jax.ShapeDtypeStruct((ROWS, PARTS * WIDE), f32),
            *[jax.ShapeDtypeStruct(part, f32)] * 3,
        ),
        in_specs=[pl.BlockSpec(memory_space=pltpu.SMEM), *[anywhere] * 6],
        out_specs=(vmem, *[anywhere] * 3),
        scratch_shapes=[
            pltpu.VMEM((2 * TOK, 32 * ROWS), bf16),
            pltpu.VMEM((ROWS, PARTS * WIDE), f32),
            pltpu.VMEM((TOK, PARTS * WIDE), bf16),
            pltpu.VMEM((PARTS * WIDE, TOK), f32),
            pltpu.VMEM((PARTS, 32, WIDE, ROWS), bf16),
            pltpu.VMEM((PARTS, WIDE, 2 * TOK), f32),
            pltpu.VMEM((PARTS, WIDE, TOK), f32),
            pltpu.VMEM((PARTS, WIDE, 2 * TOK), bf16),
            pltpu.VMEM(row, f32),
            pltpu.VMEM(row, bf16),
            pltpu.VMEM(row, bf16),
            pltpu.VMEM((PARTS, 4 // SLOTS, WIDE, SLOTS * ROWS), bf16),
            pltpu.VMEM((PARTS, 4 // SLOTS, WIDE, SLOTS * ROWS), bf16),
            pltpu.VMEM((PARTS, 2, WIDE // 2, ROWS), f32),
            pltpu.VMEM((PARTS, 2, WIDE // 2, ROWS), f32),
            pltpu.VMEM((3, 8 * QUARTER, 128), f32),
            pltpu.VMEM(part, f32),
            pltpu.VMEM(part, f32),
            pltpu.VMEM((3, QUARTER, 128), f32),
            pltpu.VMEM(part, f32),
            pltpu.VMEM((3, *part), f32),
            pltpu.SemaphoreType.DMA((7,)),
            pltpu.SemaphoreType.DMA((ARRIVALS,)),
            pltpu.SemaphoreType.DMA((3,)),
            pltpu.SemaphoreType.DMA((5,)),
            pltpu.SemaphoreType.DMA((3,)),
        ],
        compiler_params=pltpu.CompilerParams(
            collective_id=0, has_side_effects=True, vmem_limit_bytes=56 * 2**20
        ),
        name="project",
    )(index, hidden, master, key_grad, glob, local, moment)


def last_kernel(*refs):
    ins, outs, states, outer, in_sem, out_sem = refs[:7], refs[7:13], *refs[13:]
    held = [states.at[n] for n in range(4)] + [outer.at[n] for n in range(3)]
    results = [states.at[n] for n in range(4, 7)] + [outer.at[n] for n in range(3)]
    loads = [pltpu.make_async_copy(src, dst, in_sem.at[n]) for n, (src, dst) in enumerate(zip(ins, held))]
    stores = [pltpu.make_async_copy(src, dst, out_sem.at[n]) for n, (src, dst) in enumerate(zip(results, outs))]
    for load in loads:
        load.start()
    for load in loads[:4]:
        load.wait()
    gradient, weights = states[0], states[1]
    first_new = 0.9 * states[2] + 0.1 * gradient
    second_new = 0.95 * states[3] + 0.05 * gradient * gradient
    first_hat = first_new / (1.0 - 0.9**10)
    second_hat = second_new / (1.0 - 0.95**10)
    states[4] = weights - 0.01 * (first_hat / (jnp.sqrt(second_hat) + 1e-08) + 0.1 * weights)
    states[5] = first_new
    states[6] = second_new
    for store in stores[:3]:
        store.start()
    for load, store in zip(loads[4:], stores[3:]):
        load.wait()
        store.start()
    for store in stores:
        store.wait()


def last(grad, master, first, second, *outer):
    anywhere = pl.BlockSpec(memory_space=pl.ANY)
    return pl.pallas_call(
        last_kernel,
        out_shape=tuple(jax.ShapeDtypeStruct(v.shape, jnp.float32) for v in (master, first, second, *outer)),
        in_specs=[anywhere] * 7,
        out_specs=(anywhere,) * 6,
        scratch_shapes=[
            pltpu.VMEM((7, *master.shape), jnp.float32),
            pltpu.VMEM((3, *outer[0].shape), jnp.float32),
            pltpu.SemaphoreType.DMA((7,)),
            pltpu.SemaphoreType.DMA((6,)),
        ],
        compiler_params=pltpu.CompilerParams(vmem_limit_bytes=56 * 2**20),
        name="last",
    )(grad, master, first, second, *outer)


def rows_of(fragments):
    return fragments.reshape(2, -1, 128).transpose(1, 0, 2).reshape(-1, 128)


def shards(
    hidden,
    master,
    moment_first,
    moment_second,
    key_grad,
    frag_global,
    frag_local,
    frag_moment,
    frag_index,
):
    grad, *outer = project(
        frag_index,
        hidden[0],
        master[0],
        key_grad[0],
        rows_of(frag_global),
        rows_of(frag_local[0]),
        rows_of(frag_moment),
    )
    weights_new, first_new, second_new, *outer = last(grad, master[0], moment_first[0], moment_second[0], *outer)
    outer_global, outer_moment, mixed_local = (part.reshape(-1) for part in outer)
    return (
        weights_new[None],
        first_new[None],
        second_new[None],
        outer_global,
        outer_moment,
        mixed_local[None],
    )


def solution(mesh):
    placed = (
        P("replica", "fsdp", None),
        P("replica", "fsdp", None),
        P("replica", "fsdp", None),
        P("replica", "fsdp", None),
        P("replica", "fsdp", None),
        P(None, "fsdp"),
        P("replica", None, "fsdp"),
        P(None, "fsdp"),
        P(),
    )
    return jax.shard_map(
        shards,
        mesh=mesh,
        in_specs=placed,
        out_specs=(
            P("replica", "fsdp", None),
            P("replica", "fsdp", None),
            P("replica", "fsdp", None),
            P("fsdp"),
            P("fsdp"),
            P("replica", "fsdp"),
        ),
        check_vma=False,
    )
```

```python
import jax
import jax.numpy as jnp
from jax import lax
from jax.experimental import pallas as pl
from jax.experimental.pallas import tpu as pltpu
from jax.sharding import PartitionSpec as P

MESH = pl.DeviceIdType.MESH
HEAD = 128
PARTS = 2
WIDE = 256
TOK = 384
ROWS = 128
SLOTS = 1
QUARTER = 256
ARRIVALS = 120

ORDER = (
    ('zsend', 0),
    ('own', 1, 0),
    ('hids',),
    ('zsend', 1),
    ('own', 0, 0),
    ('own', 0, 1),
    ('passp', 1, 0, 0),
    ('passm', 1, 0, 0),
    ('nextm', 1, 0),
    ('rep',),
    ('passm', 0, 0, 0),
    ('passp', 0, 0, 0),
    ('nextp', 0, 0),
    ('nextm', 0, 0),
    ('passp', 0, 1, 0),
    ('passm', 0, 1, 0),
    ('hid',),
    ('kgt',),
    ('nextm', 0, 1),
    ('nextp', 0, 1),
    ('passm', 0, 0, 3),
    ('passp', 0, 0, 3),
    ('far', 0, 0),
    ('passp', 1, 0, 1),
    ('passm', 1, 0, 1),
    ('own', 1, 1),
    ('passp', 0, 1, 1),
    ('passm', 0, 1, 1),
    ('passm', 0, 0, 1),
    ('passp', 0, 0, 1),
    ('far', 0, 1),
    ('keys', 0, 0),
    ('passp', 0, 1, 3),
    ('passm', 0, 1, 3),
    ('passm', 0, 0, 2),
    ('passp', 0, 0, 2),
    ('keys', 0, 1),
    ('nextp', 1, 0),
    ('passm', 1, 1, 0),
    ('passp', 1, 1, 0),
    ('nextp', 1, 1),
    ('nextm', 1, 1),
    ('keys', 0, 3),
    ('passm', 0, 1, 2),
    ('passp', 0, 1, 2),
    ('keys', 0, 2),
    ('far', 1, 0),
    ('passp', 1, 0, 3),
    ('passm', 1, 0, 3),
    ('passm', 1, 1, 3),
    ('passp', 1, 1, 3),
    ('far', 1, 1),
    ('keys', 1, 0),
    ('keys', 0, 4),
    ('passm', 1, 1, 1),
    ('swap', 0),
    ('passp', 1, 1, 1),
    ('rep2',),
    ('passp', 1, 0, 2),
    ('passm', 1, 0, 2),
    ('keys', 1, 1),
    ('deltas', 0),
    ('passm', 1, 1, 2),
    ('passp', 1, 1, 2),
    ('keys', 1, 2),
    ('grad', 0, 2),
    ('rfar', 0, 0, 2),
    ('rfar', 0, 1, 3),
    ('rfar', 0, 1, 1),
    ('rfar', 0, 0, 0),
    ('keys', 1, 3),
    ('rfar', 0, 1, 0),
    ('rfar', 0, 0, 3),
    ('grad', 0, 0),
    ('rfar', 0, 1, 2),
    ('rfar', 0, 0, 1),
    ('keys', 1, 4),
    ('swap', 1),
    ('grad', 0, 3),
    ('rn3', 0, 0, 3),
    ('rn3', 0, 0, 0),
    ('rn3', 0, 1, 3),
    ('rn3', 0, 1, 2),
    ('grad', 0, 1),
    ('rn1', 0, 1, 2),
    ('rn1', 0, 1, 1),
    ('rn1', 0, 0, 2),
    ('rn1b', 0, 0, 2),
    ('rn3', 0, 0, 2),
    ('rn3', 0, 1, 1),
    ('rn3b', 0, 0, 2),
    ('rn1b', 0, 1, 1),
    ('deltas', 1),
    ('rn1', 0, 0, 1),
    ('rn3b', 0, 1, 1),
    ('rn3', 0, 0, 1),
    ('rn3b', 0, 1, 3),
    ('rn1', 0, 1, 0),
    ('rn1', 0, 0, 3),
    ('rn3b', 0, 0, 3),
    ('rn1b', 0, 1, 2),
    ('rn1b', 0, 0, 3),
    ('rn3b', 0, 1, 2),
    ('grad', 1, 2),
    ('rfar', 1, 0, 1),
    ('rfar', 1, 1, 2),
    ('grad', 1, 3),
    ('rfar', 1, 1, 1),
    ('rn1', 0, 1, 3),
    ('rn1b', 0, 1, 3),
    ('rfar', 1, 1, 3),
    ('rn3', 1, 0, 1),
    ('rn3', 1, 0, 2),
    ('grad', 1, 1),
    ('row', 0, 0, 2),
    ('rn1', 1, 0, 2),
    ('row', 0, 1, 1),
    ('rn1', 1, 1, 3),
    ('rn3', 1, 1, 2),
    ('rn3', 1, 1, 3),
    ('rfar', 1, 0, 2),
    ('rn1', 1, 1, 2),
    ('rn3', 1, 0, 0),
    ('grad', 1, 0),
    ('row', 0, 0, 3),
    ('row', 0, 1, 2),
    ('rn1b', 0, 1, 0),
    ('rn3b', 1, 1, 2),
    ('rn1b', 1, 1, 2),
    ('rn3b', 1, 0, 1),
    ('rn1', 1, 0, 1),
    ('rn1', 1, 1, 1),
    ('rn3', 1, 1, 1),
    ('rn3', 1, 0, 3),
    ('rn3b', 1, 1, 1),
    ('rn1b', 1, 0, 1),
    ('rn1b', 1, 1, 1),
    ('rn3', 0, 1, 0),
    ('row', 0, 1, 3),
    ('rn3b', 1, 1, 3),
    ('rn1b', 1, 1, 3),
    ('rfar', 1, 0, 3),
    ('repf',),
    ('rn3b', 1, 0, 2),
    ('rn1b', 1, 0, 2),
    ('rn1b', 0, 0, 1),
    ('rn1', 1, 0, 0),
    ('rfar', 1, 1, 0),
    ('rn3', 1, 1, 0),
    ('rn3b', 0, 1, 0),
    ('row', 1, 1, 2),
    ('zadd', 0, 2),
    ('rn1', 0, 0, 0),
    ('rn1', 1, 0, 3),
    ('rn3b', 0, 0, 1),
    ('rn3b', 0, 0, 0),
    ('rn1b', 0, 0, 0),
    ('cfar', 0),
    ('row', 1, 0, 1),
    ('row', 1, 1, 1),
    ('rn1', 1, 1, 0),
    ('rfar', 1, 0, 0),
    ('zadd', 0, 3),
    ('cn3', 0),
    ('row', 1, 1, 3),
    ('rn1b', 1, 0, 3),
    ('rn3b', 1, 0, 3),
    ('rn3b', 1, 1, 0),
    ('row', 1, 0, 2),
    ('row', 0, 1, 0),
    ('rn1b', 1, 1, 0),
    ('zadd', 1, 2),
    ('cfar', 1),
    ('row', 0, 0, 1),
    ('zadd', 0, 1),
    ('cn1', 0),
    ('cn3b', 0),
    ('cn1b', 0),
    ('row', 0, 0, 0),
    ('rn3b', 1, 0, 0),
    ('zadd', 1, 1),
    ('cn1', 1),
    ('rn1b', 1, 0, 0),
    ('row', 1, 0, 3),
    ('zadd', 1, 3),
    ('row', 1, 1, 0),
    ('cn3', 1),
    ('cn3b', 1),
    ('cn1b', 1),
    ('zadd', 0, 0),
    ('finish', 0),
    ('row', 1, 0, 0),
    ('zadd', 1, 0),
    ('finish', 1),
)


def norm_backward(keys, upstream):
    inverse = lax.rsqrt(jnp.mean(keys * keys, axis=0, keepdims=True) + 1e-06)
    normed = keys * inverse
    return inverse * (upstream - normed * jnp.mean(upstream * normed, axis=0, keepdims=True))


def kernel(
    index,
    hidden,
    master_hbm,
    key_grad_hbm,
    glob_hbm,
    local_hbm,
    moment_hbm,
    grad_out,
    global_out,
    moment_out,
    mixed_out,
    hid,
    master,
    key_grad,
    key_grad_t,
    wts,
    acc,
    acc_in,
    dlt,
    gbuf,
    stage,
    stage_in,
    z_stage,
    z_in,
    wide,
    wide_in,
    frags,
    diff,
    local,
    rep_in,
    delta,
    outer,
    send_sem,
    recv_sem,
    hid_sem,
    in_sem,
    out_sem,
):
    r = lax.axis_index("replica")
    f = lax.axis_index("fsdp")
    z, y, x, c = f // 32, (f // 8) % 4, (f // 2) % 4, f % 2

    def at(zz, yy, xx, cc):
        return (r, zz * 32 + (yy % 4) * 8 + (xx % 4) * 2 + cc)

    a_up, a_down = at(z, y + z, x + 1 - z, c), at(z, y + 4 - z, x + 3 + z, c)
    b_up, b_down = at(z, y + 1 - z, x + z, c), at(z, y + 3 + z, x + 4 - z, c)
    over_z, sibling = at(1 - z, y, x, c), at(z, y, x, 1 - c)
    reps = [((r + k) % 4, f) for k in (1, 2, 3)]
    axes = ((a_up, a_down), (b_up, b_down))

    def ways(h, t):
        return axes if (h + t) % 2 == 0 else axes[::-1]


    loads = [
        pltpu.make_async_copy(src, dst, in_sem.at[n])
        for n, (src, dst) in enumerate(
            (
                (master_hbm, master),
                (key_grad_hbm, key_grad),
                (glob_hbm, frags.at[0, pl.ds(0, 8 * QUARTER)]),
                (local_hbm, frags.at[1, pl.ds(0, 8 * QUARTER)]),
                (moment_hbm, frags.at[2, pl.ds(0, 8 * QUARTER)]),
            )
        )
    ]
    loads[0].start()
    barrier = pltpu.get_barrier_semaphore()
    peers = [a_up, a_down, b_up, b_down, over_z, sibling, *reps]
    for peer in peers:
        pl.semaphore_signal(barrier, inc=1, device_id=peer, device_id_type=MESH)

    def chip_of(n):
        t, s, q = n // 16, (n // 4) % 4, n % 4
        plane = (z + t) % 2
        yy = (y + s * (1 - plane) + q * plane) % 4
        xx = (x + q * (1 - plane) + s * plane) % 4
        return plane * 16 + yy * 4 + xx

    def columns(block):
        return pl.ds(pl.multiple_of(block * ROWS, ROWS), ROWS)

    @pl.loop(0, 32)
    def _(n):
        pltpu.make_async_copy(
            hidden.at[:, columns(2 * chip_of(n) + c)], hid.at[pl.ds(0, TOK), columns(n)], hid_sem.at[0]
        ).start()

    for load in loads[1:]:
        load.start()
    loads[0].wait()
    wts[0, 0] = master[:, :WIDE].T.astype(jnp.bfloat16)
    wts[1, 0] = master[:, WIDE:].T.astype(jnp.bfloat16)
    pl.semaphore_wait(barrier, len(peers))

    arrivals = {}

    def send(what, group, src, dst, to):
        pltpu.make_async_remote_copy(
            src_ref=src,
            dst_ref=dst,
            send_sem=send_sem.at[group],
            recv_sem=recv_sem.at[arrivals.setdefault(what, len(arrivals))],
            device_id=to,
            device_id_type=MESH,
        ).start()

    def taken(semaphore, as_large):
        pltpu.make_async_copy(as_large, as_large, semaphore).wait()

    def arrived(what, as_large):
        taken(recv_sem.at[arrivals[what]], as_large)

    gather, scatter, sums, keys_swap, delta_swap, summed, spread = range(7)

    def slot(h, t, s, q):
        return wts.at[h, 16 * t + 4 * s + q]

    lower, upper = pl.ds(0, WIDE // 2), pl.ds(WIDE // 2, WIDE // 2)

    def zsend(h):
        send(("z", h), gather, slot(h, 0, 0, 0), slot(h, 1, 0, 0), over_z)

    def over_second(h, t, q):
        _, (up, down) = ways(h, t)
        src = slot(h, t, 0, q)
        send(("s+", h, t, q), gather, src, slot(h, t, 3, q), up)
        send(("s-", h, t, q), gather, src, slot(h, t, 1, q), down)

    def own(h, t):
        (up, down), _ = ways(h, t)
        if t == 1:
            arrived(("z", h), slot(h, 1, 0, 0))
        src = slot(h, t, 0, 0)
        send(("f+", h, t), gather, src, slot(h, t, 0, 3), up)
        send(("f-", h, t), gather, src, slot(h, t, 0, 1), down)
        over_second(h, t, 0)

    def nextp(h, t):
        arrived(("f+", h, t), slot(h, t, 0, 3))
        send(("ff", h, t), gather, slot(h, t, 0, 3).at[lower], slot(h, t, 0, 2).at[lower], ways(h, t)[0][0])
        over_second(h, t, 3)

    def nextm(h, t):
        arrived(("f-", h, t), slot(h, t, 0, 1))
        send(("ff", h, t), gather, slot(h, t, 0, 1).at[upper], slot(h, t, 0, 2).at[upper], ways(h, t)[0][1])
        over_second(h, t, 1)

    def far(h, t):
        arrived(("ff", h, t), slot(h, t, 0, 2))
        over_second(h, t, 2)

    def passp(h, t, q):
        arrived(("s+", h, t, q), slot(h, t, 3, q))
        send(("ss", h, t), gather, slot(h, t, 3, q).at[lower], slot(h, t, 2, q).at[lower], ways(h, t)[1][0])

    def passm(h, t, q):
        arrived(("s-", h, t, q), slot(h, t, 1, q))
        send(("ss", h, t), gather, slot(h, t, 1, q).at[upper], slot(h, t, 2, q).at[upper], ways(h, t)[1][1])

    def hidden_of(h, rows):
        blocks = [16 * t + (4 * s + q if h == 0 else 4 * q + s) for t, s in rows for q in range(4)]
        return jnp.concatenate([hid[:, n * ROWS : (n + 1) * ROWS] for n in blocks], axis=1)

    def keys(h, n):
        rows = (((0, 0), (1, 0)), ((0, 1), (0, 3)), ((1, 1), (1, 3)), ((0, 2),), ((1, 2),))[n]
        if n >= 3:
            arrived(("ss", h, n - 3), wts.at[h, pl.ds(0, 4)])
        weights = [wts[h, 16 * t + 4 * s + q] for t, s in rows for q in range(4)]
        part = lax.dot_general(
            jnp.concatenate(weights, axis=1),
            hidden_of(h, rows),
            (((1,), (1,)), ((), ())),
            preferred_element_type=jnp.float32,
        )
        if n == 0:
            acc[h] = part
        else:
            acc[h] += part

    def swap(h):
        send(("keys", h), keys_swap, acc.at[h, :, pl.ds(TOK, TOK)], acc_in.at[h], sibling)

    def kgt():
        loads[1].wait()
        key_grad_t[...] = key_grad[...].astype(jnp.float32).T

    def deltas(h):
        arrived(("keys", h), acc_in.at[h])
        for n in range(WIDE // HEAD):
            rows, of_all = pl.ds(n * HEAD, HEAD), pl.ds(h * WIDE + n * HEAD, HEAD)
            of_head = acc[h, rows, :TOK] + acc_in[h, rows, :]
            dlt[h, rows, :TOK] = norm_backward(of_head, key_grad_t[of_all, :]).astype(jnp.bfloat16)
        send(("delta", h), delta_swap, dlt.at[h, :, pl.ds(0, TOK)], dlt.at[h, :, pl.ds(TOK, TOK)], sibling)

    low, high, both = slice(0, WIDE // 2), slice(WIDE // 2, WIDE), slice(0, WIDE)

    def grad(h, s):
        if s == 2:
            arrived(("delta", h), dlt.at[h, :, pl.ds(TOK, TOK)])
        value = jnp.dot(dlt[h], hidden_of(h, ((0, s), (1, s))), preferred_element_type=jnp.float32)
        for t in range(2):
            one = value[:, t * 4 * ROWS : (t + 1) * 4 * ROWS]
            if s == 2:
                stage[h, t, s] = one.astype(jnp.bfloat16)
            elif s == 0:
                gbuf[h, t, s] = one
            else:
                now, later = (high, low) if s == 1 else (low, high)
                stage[h, t, s, now, :] = one[now].astype(jnp.bfloat16)
                gbuf[h, t, s, later, :] = one[later]

    def cols_of(q):
        return slice(q * ROWS, (q + 1) * ROWS)

    def cols_in(k):
        return slice(k * SLOTS * ROWS, (k + 1) * SLOTS * ROWS)

    def half_of(h, t, s, k, rows):
        return (h, t, s, pl.ds(rows.start, WIDE // 2), pl.ds(k * SLOTS * ROWS, SLOTS * ROWS))

    def row_send(name, h, t, s, k, rows, to):
        where = half_of(h, t, s, k, rows)
        send((name, h, t, k), scatter, stage.at[where], stage_in.at[where], to)

    def received(h, t, s, cols, rows):
        return stage_in[h, t, s, rows, cols].astype(jnp.float32)

    def rfar(h, t, k):
        row_send("rf+", h, t, 2, k, low, ways(h, t)[1][0])
        row_send("rf-", h, t, 2, k, high, ways(h, t)[1][1])

    def rn1(h, t, k):
        row_send("r", h, t, 1, k, high, ways(h, t)[1][0])

    def rn3(h, t, k):
        row_send("r", h, t, 3, k, low, ways(h, t)[1][1])

    def rn1b(h, t, k):
        arrived(("rf+", h, t, k), stage_in.at[half_of(h, t, 2, k, low)])
        total = gbuf[h, t, 1, low, cols_in(k)] + received(h, t, 2, cols_in(k), low)
        stage[h, t, 1, low, cols_in(k)] = total.astype(jnp.bfloat16)
        row_send("r", h, t, 1, k, low, ways(h, t)[1][0])

    def rn3b(h, t, k):
        arrived(("rf-", h, t, k), stage_in.at[half_of(h, t, 2, k, high)])
        total = gbuf[h, t, 3, high, cols_in(k)] + received(h, t, 2, cols_in(k), high)
        stage[h, t, 3, high, cols_in(k)] = total.astype(jnp.bfloat16)
        row_send("r", h, t, 3, k, high, ways(h, t)[1][1])

    def row(h, t, k):
        arrived(("r", h, t, k), stage_in.at[h, t, pl.ds(0, 2), :, pl.ds(k * SLOTS * ROWS, SLOTS * ROWS)])
        cols = cols_in(k)
        total = gbuf[h, t, 0, :, cols] + received(h, t, 1, cols, both) + received(h, t, 3, cols, both)
        if t == 1:
            z_stage[h, k] = total.astype(z_stage.dtype)
            send(("zr", h, k), scatter, z_stage.at[h, k], z_in.at[h, k], over_z)
        else:
            gbuf[h, t, 0, :, cols] = total

    def zadd(h, k):
        arrived(("zr", h, k), z_in.at[h, k])
        gbuf[h, 0, 0, :, cols_in(k)] += z_in[h, k].astype(jnp.float32)

    def own_slot(h, q, rows):
        return gbuf[h, 0, 0, rows, cols_of(q)]

    def half_slot(h, q, rows):
        return (h, 0, 0, pl.ds(rows.start, WIDE // 2), pl.ds(q * ROWS, ROWS))

    def one_send(name, h, q, rows, to, value):
        stage[h, 0, 0, rows, cols_of(q)] = value.astype(jnp.bfloat16)
        where = half_slot(h, q, rows)
        send((name, h), scatter, stage.at[where], stage_in.at[where], to)

    def sum_send(h, n, to, value):
        wide[h, n] = value
        send(("sum", h), sums, wide.at[h, n], wide_in.at[h, n], to)

    def cfar(h):
        one_send("cf+", h, 2, low, ways(h, 0)[0][0], own_slot(h, 2, low))
        one_send("cf-", h, 2, high, ways(h, 0)[0][1], own_slot(h, 2, high))

    def cn1(h):
        one_send("c", h, 1, high, ways(h, 0)[0][0], own_slot(h, 1, high))

    def cn3(h):
        one_send("c", h, 3, low, ways(h, 0)[0][1], own_slot(h, 3, low))

    def cn1b(h):
        arrived(("cf+", h), stage_in.at[half_slot(h, 2, low)])
        sum_send(h, 0, ways(h, 0)[0][0], own_slot(h, 1, low) + received(h, 0, 0, cols_of(2), low))

    def cn3b(h):
        arrived(("cf-", h), stage_in.at[half_slot(h, 2, high)])
        sum_send(h, 1, ways(h, 0)[0][1], own_slot(h, 3, high) + received(h, 0, 0, cols_of(2), high))

    def finish(h):
        arrived(("c", h), stage_in.at[h, 0, 0, :, pl.ds(0, ROWS)])
        arrived(("sum", h), wide_in.at[h])
        own = own_slot(h, 0, both)
        into_low = wide_in[h, 0] + received(h, 0, 0, cols_of(3), low)
        into_high = received(h, 0, 0, cols_of(1), high) + wide_in[h, 1]
        grad_out[:, h * WIDE : h * WIDE + WIDE // 2] = (own[low] + into_low).T
        grad_out[:, h * WIDE + WIDE // 2 : (h + 1) * WIDE] = (own[high] + into_high).T

    def hids():
        @pl.loop(0, 32)
        def _(n):
            pltpu.make_async_remote_copy(
                src_ref=hidden.at[:, columns(2 * chip_of(n) + 1 - c)],
                dst_ref=hid.at[pl.ds(TOK, TOK), columns(n)],
                send_sem=hid_sem.at[1],
                recv_sem=hid_sem.at[2],
                device_id=sibling,
                device_id_type=MESH,
            ).start()

    mine, theirs = hid.at[pl.ds(0, TOK)], hid.at[pl.ds(TOK, TOK)]

    def hid_wait():
        taken(hid_sem.at[0], mine)
        taken(hid_sem.at[2], theirs)

    def chosen(n, rows):
        first = frags[n, pl.ds(2 * rows.start, rows.size, stride=2), :]
        second = frags[n, pl.ds(2 * rows.start + 1, rows.size, stride=2), :]
        return jnp.where(index[0] == 0, first, second)

    def rep():
        loads[2].wait()
        loads[3].wait()
        for n in range(4):
            rows = pl.ds(n * QUARTER, QUARTER)
            own_local = chosen(1, rows)
            local[rows, :] = own_local
            diff[rows, :] = chosen(0, rows) - own_local
        for k, to in zip((1, 2, 3), reps):
            send("rep", summed, diff.at[pl.ds(((r + k) % 4) * QUARTER, QUARTER)], rep_in.at[k - 1], to)

    def rep2():
        arrived("rep", rep_in)
        own_rows = pl.ds(r * QUARTER, QUARTER)
        delta[own_rows, :] = (diff[own_rows, :] + rep_in[0] + rep_in[1] + rep_in[2]) * 0.25
        for k, to in zip((1, 2, 3), reps):
            send("rep out", spread, delta.at[own_rows], delta.at[own_rows], to)

    stores = [
        pltpu.make_async_copy(outer.at[n], dst, out_sem.at[n])
        for n, dst in enumerate((global_out, moment_out, mixed_out))
    ]

    def repf():
        loads[4].wait()
        arrived("rep out", rep_in)
        for n in range(4):
            rows = pl.ds(n * QUARTER, QUARTER)
            step = delta[rows, :]
            outer_moment = 0.9 * chosen(2, rows) + step
            outer_global = chosen(0, rows) - 0.7 * (0.9 * outer_moment + step)
            outer[0, rows, :] = outer_global
            outer[1, rows, :] = outer_moment
            outer[2, rows, :] = 0.5 * local[rows, :] + 0.5 * outer_global
        for store in stores:
            store.start()

    steps = dict(
        zsend=zsend, own=own, nextp=nextp, nextm=nextm, far=far, passp=passp, passm=passm, keys=keys, swap=swap,
        deltas=deltas, grad=grad, rfar=rfar, rn1=rn1, rn3=rn3, rn1b=rn1b, rn3b=rn3b, row=row, zadd=zadd, cfar=cfar,
        cn1=cn1, cn3=cn3, cn1b=cn1b, cn3b=cn3b, finish=finish, hids=hids, hid=hid_wait, kgt=kgt, rep=rep, rep2=rep2, repf=repf,
    )
    for name, *where in ORDER:
        steps[name](*where)
    assert len(arrivals) == ARRIVALS
    for group, as_large in (
        (gather, wts.at[:, pl.ds(0, 31)]),
        (scatter, wts.at[:, pl.ds(0, 30)]),
        (sums, wide_in),
        (keys_swap, acc_in),
        (delta_swap, dlt.at[:, :, pl.ds(0, TOK)]),
        (summed, rep_in),
        (spread, rep_in),
    ):
        taken(send_sem.at[group], as_large)
    taken(hid_sem.at[1], mine)
    for store in stores:
        store.wait()


def project(index, hidden, master, key_grad, glob, local, moment):
    vmem, anywhere = pl.BlockSpec(memory_space=pltpu.VMEM), pl.BlockSpec(memory_space=pl.ANY)
    f32, bf16 = jnp.float32, jnp.bfloat16
    part = (4 * QUARTER, 128)
    row = (PARTS, 2, 4, WIDE, 4 * ROWS)
    return pl.pallas_call(
        kernel,
        out_shape=(
            jax.ShapeDtypeStruct((ROWS, PARTS * WIDE), f32),
            *[jax.ShapeDtypeStruct(part, f32)] * 3,
        ),
        in_specs=[pl.BlockSpec(memory_space=pltpu.SMEM), *[anywhere] * 6],
        out_specs=(vmem, *[anywhere] * 3),
        scratch_shapes=[
            pltpu.VMEM((2 * TOK, 32 * ROWS), bf16),
            pltpu.VMEM((ROWS, PARTS * WIDE), f32),
            pltpu.VMEM((TOK, PARTS * WIDE), bf16),
            pltpu.VMEM((PARTS * WIDE, TOK), f32),
            pltpu.VMEM((PARTS, 32, WIDE, ROWS), bf16),
            pltpu.VMEM((PARTS, WIDE, 2 * TOK), f32),
            pltpu.VMEM((PARTS, WIDE, TOK), f32),
            pltpu.VMEM((PARTS, WIDE, 2 * TOK), bf16),
            pltpu.VMEM(row, f32),
            pltpu.VMEM(row, bf16),
            pltpu.VMEM(row, bf16),
            pltpu.VMEM((PARTS, 4 // SLOTS, WIDE, SLOTS * ROWS), bf16),
            pltpu.VMEM((PARTS, 4 // SLOTS, WIDE, SLOTS * ROWS), bf16),
            pltpu.VMEM((PARTS, 2, WIDE // 2, ROWS), f32),
            pltpu.VMEM((PARTS, 2, WIDE // 2, ROWS), f32),
            pltpu.VMEM((3, 8 * QUARTER + 8, 128), f32),
            pltpu.VMEM(part, f32),
            pltpu.VMEM(part, f32),
            pltpu.VMEM((3, QUARTER, 128), f32),
            pltpu.VMEM(part, f32),
            pltpu.VMEM((3, *part), f32),
            pltpu.SemaphoreType.DMA((7,)),
            pltpu.SemaphoreType.DMA((ARRIVALS,)),
            pltpu.SemaphoreType.DMA((3,)),
            pltpu.SemaphoreType.DMA((5,)),
            pltpu.SemaphoreType.DMA((3,)),
        ],
        compiler_params=pltpu.CompilerParams(
            collective_id=0, has_side_effects=True, vmem_limit_bytes=56 * 2**20
        ),
        name="project",
    )(index, hidden, master, key_grad, glob, local, moment)


def last_kernel(*refs):
    ins, outs, states, outer, in_sem, out_sem = refs[:7], refs[7:13], *refs[13:]
    held = [states.at[n] for n in range(4)] + [outer.at[n] for n in range(3)]
    results = [states.at[n] for n in range(4, 7)] + [outer.at[n] for n in range(3)]
    loads = [pltpu.make_async_copy(src, dst, in_sem.at[n]) for n, (src, dst) in enumerate(zip(ins, held))]
    stores = [pltpu.make_async_copy(src, dst, out_sem.at[n]) for n, (src, dst) in enumerate(zip(results, outs))]
    for load in loads:
        load.start()
    for load in loads[:4]:
        load.wait()
    gradient, weights = states[0], states[1]
    first_new = 0.9 * states[2] + 0.1 * gradient
    second_new = 0.95 * states[3] + 0.05 * gradient * gradient
    first_hat = first_new / (1.0 - 0.9**10)
    second_hat = second_new / (1.0 - 0.95**10)
    states[4] = weights - 0.01 * (first_hat / (jnp.sqrt(second_hat) + 1e-08) + 0.1 * weights)
    states[5] = first_new
    states[6] = second_new
    for store in stores[:3]:
        store.start()
    for load, store in zip(loads[4:], stores[3:]):
        load.wait()
        store.start()
    for store in stores:
        store.wait()


def last(grad, master, first, second, *outer):
    anywhere = pl.BlockSpec(memory_space=pl.ANY)
    return pl.pallas_call(
        last_kernel,
        out_shape=tuple(jax.ShapeDtypeStruct(v.shape, jnp.float32) for v in (master, first, second, *outer)),
        in_specs=[anywhere] * 7,
        out_specs=(anywhere,) * 6,
        scratch_shapes=[
            pltpu.VMEM((7, *master.shape), jnp.float32),
            pltpu.VMEM((3, *outer[0].shape), jnp.float32),
            pltpu.SemaphoreType.DMA((7,)),
            pltpu.SemaphoreType.DMA((6,)),
        ],
        compiler_params=pltpu.CompilerParams(vmem_limit_bytes=56 * 2**20),
        name="last",
    )(grad, master, first, second, *outer)


def rows_of(fragments):
    return fragments.reshape(2, -1, 128).transpose(1, 0, 2).reshape(-1, 128)


def shards(
    hidden,
    master,
    moment_first,
    moment_second,
    key_grad,
    frag_global,
    frag_local,
    frag_moment,
    frag_index,
):
    grad, *outer = project(
        frag_index,
        hidden[0],
        master[0],
        key_grad[0],
        rows_of(frag_global),
        rows_of(frag_local[0]),
        rows_of(frag_moment),
    )
    weights_new, first_new, second_new, *outer = last(grad, master[0], moment_first[0], moment_second[0], *outer)
    outer_global, outer_moment, mixed_local = (part.reshape(-1) for part in outer)
    return (
        weights_new[None],
        first_new[None],
        second_new[None],
        outer_global,
        outer_moment,
        mixed_local[None],
    )


def solution(mesh):
    placed = (
        P("replica", "fsdp", None),
        P("replica", "fsdp", None),
        P("replica", "fsdp", None),
        P("replica", "fsdp", None),
        P("replica", "fsdp", None),
        P(None, "fsdp"),
        P("replica", None, "fsdp"),
        P(None, "fsdp"),
        P(),
    )
    return jax.shard_map(
        shards,
        mesh=mesh,
        in_specs=placed,
        out_specs=(
            P("replica", "fsdp", None),
            P("replica", "fsdp", None),
            P("replica", "fsdp", None),
            P("fsdp"),
            P("fsdp"),
            P("replica", "fsdp"),
        ),
        check_vma=False,
    )
```
